256 devices in a mesh: wide: 64 (over x, z, y_hi), narrow: 4 (over y_lo, core).
Axes of the slice: x: 4, y: 4 (y_hi: 2, y_lo: 2; y = y_hi * 2 + y_lo), z: 8, core: 2. Of those that a mesh axis runs over, the one named last changes fastest.
Arguments:
- images: bfloat16 [1024, 14, 14, 1024], P(('wide', 'narrow')), may hold values from -6 to 6
- dw_weight: float32 [7, 7, 1024], replicated, may hold values from -0.875 to 0.875
- dw_bias: float32 [1024], replicated, may hold values from -3 to 3
- ln_gain: float32 [1024], replicated, may hold values from 0.25 to 1.75
- ln_bias: float32 [1024], replicated, may hold values from -3 to 3
- w_in: bfloat16 [1024, 2048], P(None, ('wide', 'narrow')), may hold values from -0.1875 to 0.1875
- b_in: bfloat16 [2048], P(('wide', 'narrow')), may hold values from -3 to 3
- gamma: float32 [512], replicated, may hold values from 0.3 to 1
- curv_root: float32 [1024, 14, 14, 512], P(('wide', 'narrow')), may hold values from -24 to 24
- directions: float32 [2048, 1, 512], P(('wide', 'narrow')), may hold values from -30 to 30
Outputs:
- estimate: float32 [2048, 1, 512], P(('wide', 'narrow'))
The draws below stay inside these ranges and needn't reach their ends.
All inputs are finite; a program needn't handle non-finite values.
Results may differ from the reference program's by a relative error of at most 0.0032.
Values may be sent and summed in bfloat16 or wider, within the bound.
A program may use at most 64 MiB of HBM per device.

```python
import math
import jax
import jax.numpy as jnp
from jax import lax

C = 1024
HID = 2048
OUTC = 512
SIDE = 14
KER = 7
DIRS = 1
ITERS = 1
IMAGES = 1024
CELLS = 196


def draw_directions(key, part):
    key = jax.random.fold_in(key, 7)
    key_base, key_cols = jax.random.split(key, 2)
    row_scale = 10.0 ** (jnp.arange(HID, dtype=jnp.float32) / (HID - 1))
    col_scale = jnp.exp(jax.random.uniform(key_cols, (OUTC,), jnp.float32, 0.0, math.log(10.0)))
    base = jax.random.truncated_normal(key_base, -6.0, 6.0, (HID, DIRS, OUTC), jnp.float32)
    return (0.05 * base * row_scale[:, None, None] * col_scale[None, None, :]).astype(jnp.float32)


def raised(entries, own_key, source, target, blocks, factor):
    def block_of(axis_at):
        return (jnp.arange(entries.shape[axis_at]) // (entries.shape[axis_at] // blocks)).reshape((-1,) + (1,) * (entries.ndim - 1 - axis_at))

    one_side = jax.random.permutation(own_key, blocks)[block_of(target)]
    second = (block_of(target) + blocks // 2) % blocks
    return jnp.where((block_of(source) == one_side) | (block_of(source) == second), factor * entries, entries)


def shard_levels(stream_key, shape, cuts, least, largest):
    loudness = 1.0
    for position, shards_of in cuts:
        draws = jax.random.uniform(jax.random.fold_in(jax.random.fold_in(stream_key, 6), position), (shards_of,), jnp.float32, least / len(cuts), largest / len(cuts))
        loudness = loudness * jnp.repeat(jnp.exp(draws), shape[position] // shards_of).reshape((-1,) + (1,) * (len(shape) - 1 - position))
    return loudness


def centred(stream_key, dims, width, reach, cuts=(), kind=jnp.bfloat16):
    gain = shard_levels(stream_key, dims, cuts, -0.22, 0.18) if cuts else 1.0
    array = jax.random.normal(stream_key, dims, jnp.float32) * width * gain
    return jnp.minimum(jnp.maximum(array, -reach), reach).astype(kind)


def gaussian_with(key, dims, width, most, shards, heavy, kind=jnp.bfloat16):
    result = width * jax.random.normal(key, dims, jnp.float32)
    if shards:
        result = result * shard_levels(key, dims, shards, -0.22, 0.18)
    return jnp.clip(raised(result, jax.random.fold_in(key, 3), *heavy), -most, most).astype(kind)


def setup_inputs(seed: int = 0) -> dict:
    key_of = jax.random.split(jax.random.key(seed), 11)
    images = centred(key_of[0], (IMAGES, SIDE, SIDE, C), 1.0, 6.0, ((0, 256),))
    dw_weight = centred(key_of[1], (KER, KER, C), (KER * KER) ** -0.5, 0.875, (), jnp.float32)
    dw_bias = centred(key_of[2], (C,), 0.5, 3.0, (), jnp.float32)
    ln_gain = jnp.clip(1.0 + 0.15 * jax.random.normal(key_of[3], (C,), jnp.float32), 0.25, 1.75)
    ln_bias = centred(key_of[4], (C,), 0.5, 3.0, (), jnp.float32)
    w_in = centred(key_of[5], (C, HID), C ** -0.5, 0.1875, ((1, 256),))
    b_in = centred(key_of[6], (HID,), 0.5, 3.0, ((0, 256),))
    gamma = jnp.clip(jnp.exp(jax.random.uniform(key_of[7], (OUTC,), jnp.float32, math.log(0.3), math.log(1.0))), 0.3, 1.0)
    curv_root = gaussian_with(key_of[8], (IMAGES, SIDE, SIDE, OUTC), 1.0, 24.0, ((0, 256),), (0, 3, 256, 6.0), jnp.float32)
    directions = draw_directions(jax.random.fold_in(key_of[10], 71), 0)
    return dict(images=images, dw_weight=dw_weight, dw_bias=dw_bias, ln_gain=ln_gain, ln_bias=ln_bias, w_in=w_in, b_in=b_in, gamma=gamma, curv_root=curv_root, directions=directions)


damping = 0.05
scale_coef = 0.4
clip_ratio = 1.2

def centre(values, axis):
    return values - lax.optimization_barrier(jnp.mean(values, axis=axis, keepdims=True))

def features(images, dw_weight, dw_bias, ln_gain, ln_bias):
    channels = images.shape[3]
    kernel = dw_weight.reshape(dw_weight.shape[0], dw_weight.shape[1], 1, channels)
    mixed = lax.conv_general_dilated(images.astype(jnp.float32), kernel, (1, 1), 'SAME', dimension_numbers=('NHWC', 'HWIO', 'NHWC'), feature_group_count=channels, precision=lax.Precision.HIGHEST) + dw_bias
    average = lax.optimization_barrier(jnp.mean(mixed, axis=3, keepdims=True))
    variance = lax.optimization_barrier(jnp.mean(jnp.square(mixed - average), axis=3, keepdims=True))
    normed = (mixed - average) * lax.rsqrt(variance + 1e-06) * ln_gain + ln_bias
    return normed.astype(jnp.bfloat16).reshape(images.shape[0], -1, channels)

def weights(cell_out, curvature, gamma):
    inner = curvature[:, None] * centre(cell_out, 2)
    return (centre(inner, 2) * (gamma * gamma)).astype(jnp.bfloat16)

def reference(images, dw_weight, dw_bias, ln_gain, ln_bias, w_in, b_in, gamma, curv_root, directions):

    def hidden_block(block_images):
        normed = features(block_images, dw_weight, dw_bias, ln_gain, ln_bias)
        pre = jnp.einsum('ncd,dh->nch', normed.astype(jnp.float32), w_in.astype(jnp.float32)) + b_in.astype(jnp.float32)
        return jax.nn.gelu(pre, approximate=False).astype(jnp.bfloat16)
    hidden = lax.map(hidden_block, images.reshape(IMAGES // 8, 8, SIDE, SIDE, C))
    curvature = (0.25 + curv_root * curv_root).reshape(IMAGES // 8, 8, CELLS, OUTC)
    direction_sq = lax.optimization_barrier(jnp.sum(directions * directions, axis=(0, 2)))
    estimate = directions
    for iteration in range(ITERS):
        rounded = lax.optimization_barrier(estimate.astype(jnp.bfloat16)).astype(jnp.float32)

        def accumulate(total, block):
            hidden_b, curv_b = block
            hid_float = hidden_b.astype(jnp.float32)
            cell_out = jnp.einsum('nch,hdk->ndck', hid_float, rounded)
            cell_weight = lax.optimization_barrier(weights(cell_out, curv_b, gamma)).astype(jnp.float32)
            return (total + jnp.einsum('nch,ndck->hdk', hid_float, cell_weight), None)
        product, unused = lax.scan(accumulate, jnp.zeros(directions.shape, jnp.float32), (hidden, curvature))
        fresh = directions + (1.0 - damping) * estimate - product / (scale_coef * IMAGES * CELLS)
        fresh_sq = lax.optimization_barrier(jnp.sum(fresh * fresh, axis=(0, 2)))
        factor = jnp.minimum(1.0, clip_ratio * jnp.sqrt(direction_sq / (fresh_sq + 1e-06)))
        estimate = fresh * factor[None, :, None]
    return estimate
```

```python
import jax
import jax.numpy as jnp
from jax import lax
from jax.experimental import pallas as pl
from jax.experimental.pallas import tpu as pltpu
from jax.sharding import PartitionSpec as P

damping = 0.05
scale_coef = 0.4
clip_ratio = 1.2

MESH = pl.DeviceIdType.MESH
F32 = jnp.float32
BF16 = jnp.bfloat16

CH = 1024
HID = 2048
OUTC = 512
SIDE = 14
PAD = 16
IMGS = 4
CELLS = SIDE * SIDE
ROWS = IMGS * SIDE * PAD
ALL_CELLS = 1024 * CELLS
UNITS = 8
BLOCK = 64
WROWS = 8 * BLOCK + 16
DROWS = 4 * BLOCK
TILE = 256


def features(images, dw_weight, dw_bias, ln_gain, ln_bias):
    channels = images.shape[3]
    kernel = dw_weight.reshape(dw_weight.shape[0], dw_weight.shape[1], 1, channels)
    mixed = (
        lax.conv_general_dilated(
            images.astype(F32),
            kernel,
            (1, 1),
            "SAME",
            dimension_numbers=("NHWC", "HWIO", "NHWC"),
            feature_group_count=channels,
            precision=lax.Precision.HIGHEST,
        )
        + dw_bias
    )
    average = jnp.mean(mixed, axis=3, keepdims=True)
    variance = jnp.mean(jnp.square(mixed - average), axis=3, keepdims=True)
    normed = (mixed - average) * lax.rsqrt(variance + 1e-06) * ln_gain + ln_bias
    return normed.astype(BF16)


def gelu(pre):
    return 0.5 * pre * (1.0 + lax.erf(pre * 0.7071067811865476))


def body(
    normed_ref,
    wz_ref,
    gamma_ref,
    curv_ref,
    dir_ref,
    out_ref,
    wz,
    dz,
    wbuf,
    dbuf,
    hidden,
    cell_out,
    curvature,
    cell_weight,
    pair_send,
    pair_recv,
    slab_send,
    slab_recv,
    total,
    block_send,
    block_recv,
    row_send,
    row_recv,
    sums,
    sums_recv,
    wide_sums,
    wide_recv,
    send,
    recv,
):
    wide = lax.axis_index("wide")
    narrow = lax.axis_index("narrow")
    x = wide // 16
    z = (wide // 2) % 8
    y = (wide % 2) * 2 + narrow // 2
    c = narrow % 2
    a3 = x + c * (y - x)
    a2 = y + c * (x - y)

    def at(x_, y_, z_, c_):
        return ((x_ * 8 + z_) * 2 + y_ // 2, (y_ % 2) * 2 + c_)

    def along(a3_, a2_, z_):
        return at(a3_ + c * (a2_ - a3_), a2_ + c * (a3_ - a2_), z_, c)

    sibling = at(x, y, z, 1 - c)

    def group_of(k):
        spot = (z * 2 + c + k) % 16
        return at(x, y, spot // 2, spot % 2)

    def plane_of(k):
        spot = (x * 4 + y + k) % 16
        return at(spot // 4, spot % 4, z, c)

    def remote(src, dst, sem, device):
        return pltpu.make_async_remote_copy(
            src_ref=src,
            dst_ref=dst,
            send_sem=send.at[sem],
            recv_sem=recv.at[sem],
            device_id=device,
            device_id_type=MESH,
        )

    def arrived(sem, ref):
        pltpu.make_async_copy(ref, ref, recv.at[sem]).wait()

    def left(sem, ref):
        pltpu.make_async_copy(ref, ref, send.at[sem]).wait()

    barrier = pltpu.get_barrier_semaphore()
    for k in range(1, 16):
        pl.semaphore_signal(barrier, inc=1, device_id=group_of(k), device_id_type=MESH)
        pl.semaphore_signal(barrier, inc=1, device_id=plane_of(k), device_id_type=MESH)

    wz[z] = wz_ref[...]
    own = dir_ref[...]
    dz[z] = jnp.concatenate([own[:, :256], own[:, 256:]], axis=0).astype(BF16)

    pl.semaphore_wait(barrier, 30)

    def gather_z(buf, sem):
        for k in range(1, 8):
            remote(buf.at[z], buf.at[z], sem, along(a3, a2, (z + k) % 8)).start()

    def gather_a2(buf, sem):
        for k in range(1, 4):
            place = buf.at[c, a3, a2]
            remote(place, place, sem, along(a3, (a2 + k) % 4, z)).start()

    def slab(buf, off):
        return buf.at[c, (a3 + off) % 4]

    def to_sibling(buf, off, sem):
        remote(slab(buf, off), slab(buf, off), sem, sibling).start()

    def gather_a3(buf, sem):
        remote(slab(buf, 0), slab(buf, 0), sem, along((a3 + 1) % 4, a2, z)).start()
        remote(slab(buf, 0), slab(buf, 0), sem + 1, along((a3 + 3) % 4, a2, z)).start()
        to_sibling(buf, 0, sem + 4)

    def forward_low(buf, sem):
        arrived(sem, slab(buf, 3))
        part = buf.at[c, (a3 + 3) % 4, pl.ds(0, 2)]
        remote(part, part, sem + 2, along((a3 + 1) % 4, a2, z)).start()
        to_sibling(buf, 3, sem + 7)

    def forward_high(buf, sem):
        arrived(sem + 1, slab(buf, 1))
        part = buf.at[c, (a3 + 1) % 4, pl.ds(2, 2)]
        remote(part, part, sem + 3, along((a3 + 3) % 4, a2, z)).start()
        to_sibling(buf, 1, sem + 5)

    def forward_last(buf, sem):
        arrived(sem + 2, buf.at[c, (a3 + 2) % 4, pl.ds(0, 2)])
        arrived(sem + 3, buf.at[c, (a3 + 2) % 4, pl.ds(2, 2)])
        to_sibling(buf, 2, sem + 6)

    def slab_from_sibling(buf, off, sem):
        arrived(sem + 4 + off, buf.at[1 - c, (a2 + off) % 4])

    def drain(buf, zbuf, base):
        left(base, zbuf.at[pl.ds(0, 7)])
        left(base + 1, buf.at[0, 0, pl.ds(0, 3)])
        left(base + 2, buf.at[0, 0])
        left(base + 3, buf.at[0, 0])
        left(base + 4, buf.at[0, 0, pl.ds(0, 2)])
        left(base + 5, buf.at[0, 0, pl.ds(0, 2)])
        for off in range(4):
            left(base + 6 + off, buf.at[0, 0])

    def unpack_w():
        raw = wz[...].astype(F32)
        halves = (raw[:, :8, :512].reshape(BLOCK, 512), raw[:, 8:, :512].reshape(BLOCK, 512))
        for k in range(8):
            piece = halves[k // 4][:, (k % 4) * 128 : (k % 4 + 1) * 128]
            wbuf[c, a3, a2, pl.ds(k * BLOCK, BLOCK), :] = piece.astype(BF16)
        bias = raw[:, :8, 512:].reshape(BLOCK, 128)
        row_at = lax.broadcasted_iota(jnp.int32, (BLOCK, 128), 0)
        lane_at = lax.broadcasted_iota(jnp.int32, (BLOCK, 128), 1) % BLOCK
        line = jnp.sum(jnp.where(row_at == lane_at, bias, 0.0), axis=0, keepdims=True)
        wbuf[c, a3, a2, pl.ds(8 * BLOCK, 16), :] = jnp.broadcast_to(line, (16, 128)).astype(BF16)

    def unpack_d():
        raw = dz[...].astype(F32)
        halves = (raw[:, :8].reshape(BLOCK, 256), raw[:, 8:].reshape(BLOCK, 256))
        for k in range(4):
            piece = halves[k // 2][:, (k % 2) * 128 : (k % 2 + 1) * 128]
            dbuf[c, a3, a2, pl.ds(k * BLOCK, BLOCK), :] = piece.astype(BF16)

    order = [(0, 0), (1, 0), (0, 3), (1, 3), (0, 1), (1, 1), (0, 2), (1, 2)]

    def spot(p):
        half, off = order[p]
        if half == 0:
            return c, (a3 + off) % 4
        return 1 - c, (a2 + off) % 4

    def weight_tile(p):
        h, s = spot(p)
        return jnp.concatenate(
            [wbuf[h, s, :, k * BLOCK : (k + 1) * BLOCK, :].reshape(TILE, 128) for k in range(8)], axis=1
        )

    def bias_tile(p):
        h, s = spot(p)
        rows = wbuf[h, s, :, 8 * BLOCK :, :].astype(F32)
        lane = lax.broadcasted_iota(jnp.int32, (16, 128), 1)
        lines = [jnp.where(lane < BLOCK, rows[2 * k], rows[2 * k + 1])[:1] for k in range(2)]
        return jnp.concatenate(lines, axis=1)

    def direction_tile(p):
        h, s = spot(p)
        return jnp.concatenate(
            [dbuf[h, s, :, k * BLOCK : (k + 1) * BLOCK, :].reshape(TILE, 128) for k in range(4)], axis=1
        )

    W, D = 0, 10
    gather_z(wz, W)
    gather_z(dz, D)

    @pl.loop(0, IMGS)
    def _(i):
        root = curv_ref[i]
        curvature[i, :, 0:SIDE, :] = 0.25 + root * root
        curvature[i, :, SIDE:PAD, :] = jnp.zeros((SIDE, PAD - SIDE, OUTC), F32)

    arrived(W, wz.at[pl.ds(0, 7)])
    unpack_w()
    gather_a2(wbuf, W + 1)
    arrived(D, dz.at[pl.ds(0, 7)])
    unpack_d()
    gather_a2(dbuf, D + 1)
    arrived(W + 1, wbuf.at[0, 0, pl.ds(0, 3)])
    gather_a3(wbuf, W + 2)
    arrived(D + 1, dbuf.at[0, 0, pl.ds(0, 3)])
    forward_low(wbuf, W + 2)
    forward_high(wbuf, W + 2)
    gather_a3(dbuf, D + 2)

    def project(p):
        pre = lax.dot_general(
            normed_ref[...], weight_tile(p), (((1,), (1,)), ((), ())), preferred_element_type=F32
        )
        hidden[:, p * TILE : (p + 1) * TILE] = gelu(pre + bias_tile(p)).astype(BF16)

    project(0)
    slab_from_sibling(wbuf, 0, W + 2)
    project(1)
    forward_last(wbuf, W + 2)
    project(2)
    slab_from_sibling(wbuf, 3, W + 2)
    project(3)
    forward_low(dbuf, D + 2)
    forward_high(dbuf, D + 2)
    project(4)
    slab_from_sibling(wbuf, 1, W + 2)
    project(5)
    project(6)
    slab_from_sibling(wbuf, 2, W + 2)
    project(7)
    forward_last(dbuf, D + 2)
    for off in range(4):
        slab_from_sibling(dbuf, off, D + 2)

    directions = jnp.concatenate([direction_tile(p) for p in range(8)], axis=0)
    cell_out[...] = jnp.dot(hidden[...], directions, preferred_element_type=F32).reshape(
        IMGS, SIDE, PAD, OUTC
    )

    scale = gamma_ref[...] * gamma_ref[...]

    @pl.loop(0, IMGS)
    def _(i):
        inside = lax.broadcasted_iota(jnp.int32, (SIDE, PAD, OUTC), 1) < SIDE
        values = jnp.where(inside, cell_out[i], 0.0)
        mean = jnp.sum(values, axis=(0, 1), keepdims=True) * (1.0 / CELLS)
        inner = curvature[i] * (values - mean)
        again = jnp.sum(inner, axis=(0, 1), keepdims=True) * (1.0 / CELLS)
        final = jnp.where(inside, (inner - again) * scale[None], 0.0)
        cell_weight[i] = final.astype(BF16)

    def product(p):
        return lax.dot_general(
            hidden[:, p * TILE : (p + 1) * TILE],
            cell_weight[...].reshape(ROWS, OUTC),
            (((0,), (0,)), ((), ())),
            preferred_element_type=F32,
        )

    R = 20
    for off in (2, 1, 3, 0):
        pair_send[off] = product(order.index((1, off))).astype(BF16)
        remote(pair_send.at[off], pair_recv.at[off], R + off, sibling).start()
    for off in (2, 1, 3):
        part = product(order.index((0, off)))
        arrived(R + off, pair_recv.at[off])
        slab_send[off - 1] = (part + pair_recv[off].astype(F32)).astype(BF16)
        remote(
            slab_send.at[off - 1], slab_recv.at[off - 1], R + 3 + off, along((a3 + off) % 4, a2, z)
        ).start()
    part = product(order.index((0, 0)))
    arrived(R, pair_recv.at[0])
    part = part + pair_recv[0].astype(F32)
    for off in (1, 2, 3):
        arrived(R + 3 + off, slab_recv.at[off - 1])
        part = part + slab_recv[off - 1].astype(F32)
    total[...] = part.reshape(4, BLOCK, OUTC)
    for off in (2, 1, 3):
        block_send[off - 1] = total[(a2 + off) % 4].astype(BF16)
        remote(
            block_send.at[off - 1], block_recv.at[off - 1], R + 6 + off, along(a3, (a2 + off) % 4, z)
        ).start()
    part = total[a2]
    for off in (1, 2, 3):
        arrived(R + 6 + off, block_recv.at[off - 1])
        part = part + block_recv[off - 1].astype(F32)
    row_send[...] = part.reshape(8, UNITS, OUTC)
    for k in (4, 3, 5, 2, 6, 1, 7):
        remote(
            row_send.at[(z + k) % 8], row_recv.at[k - 1], R + 10, along(a3, a2, (z + k) % 8)
        ).start()
    arrived(R + 10, row_recv)
    summed = row_send[z] + jnp.sum(row_recv[...], axis=0)

    estimate = dir_ref[...]
    fresh = estimate + (1.0 - damping) * estimate - summed * (1.0 / (scale_coef * ALL_CELLS))
    fresh_part = jnp.sum(fresh * fresh, axis=(0, 1), keepdims=True)
    direction_part = jnp.sum(estimate * estimate, axis=(0, 1), keepdims=True)
    row = lax.broadcasted_iota(jnp.int32, (8, 128), 0)
    sums[...] = jnp.where(row < 4, fresh_part, direction_part)
    for k in range(1, 16):
        remote(sums, sums_recv.at[k - 1], R + 11, group_of(k)).start()
    arrived(R + 11, sums_recv)
    wide_sums[...] = sums[...] + jnp.sum(sums_recv[...], axis=0)
    for k in range(1, 16):
        remote(wide_sums, wide_recv.at[k - 1], R + 12, plane_of(k)).start()
    arrived(R + 12, wide_recv)
    sq = wide_sums[...] + jnp.sum(wide_recv[...], axis=0)
    fresh_sq = sq[0:1, 0:1]
    direction_sq = sq[4:5, 0:1]
    factor = jnp.minimum(1.0, clip_ratio * jnp.sqrt(direction_sq / (fresh_sq + 1e-06)))
    out_ref[...] = fresh * factor

    drain(wbuf, wz, W)
    drain(dbuf, dz, D)
    for off in range(4):
        left(R + off, pair_send.at[off])
    for off in range(1, 4):
        left(R + 3 + off, slab_send.at[off - 1])
        left(R + 6 + off, block_send.at[off - 1])
    left(R + 10, row_recv)
    left(R + 11, sums_recv)
    left(R + 12, wide_recv)


def step(normed, wz, gamma, curv_root, directions):
    vmem = pl.BlockSpec(memory_space=pltpu.VMEM)
    return pl.pallas_call(
        body,
        out_shape=jax.ShapeDtypeStruct((UNITS, OUTC), F32),
        in_specs=[vmem] * 5,
        out_specs=vmem,
        scratch_shapes=[
            pltpu.VMEM((8, 16, 640), BF16),
            pltpu.VMEM((8, 16, 256), BF16),
            pltpu.VMEM((2, 4, 4, WROWS, 128), BF16),
            pltpu.VMEM((2, 4, 4, DROWS, 128), BF16),
            pltpu.VMEM((ROWS, HID), BF16),
            pltpu.VMEM((IMGS, SIDE, PAD, OUTC), F32),
            pltpu.VMEM((IMGS, SIDE, PAD, OUTC), F32),
            pltpu.VMEM((IMGS, SIDE, PAD, OUTC), BF16),
            pltpu.VMEM((4, TILE, OUTC), BF16),
            pltpu.VMEM((4, TILE, OUTC), BF16),
            pltpu.VMEM((3, TILE, OUTC), BF16),
            pltpu.VMEM((3, TILE, OUTC), BF16),
            pltpu.VMEM((4, BLOCK, OUTC), F32),
            pltpu.VMEM((3, BLOCK, OUTC), BF16),
            pltpu.VMEM((3, BLOCK, OUTC), BF16),
            pltpu.VMEM((8, UNITS, OUTC), F32),
            pltpu.VMEM((7, UNITS, OUTC), F32),
            pltpu.VMEM((8, 128), F32),
            pltpu.VMEM((15, 8, 128), F32),
            pltpu.VMEM((8, 128), F32),
            pltpu.VMEM((15, 8, 128), F32),
            pltpu.SemaphoreType.DMA((40,)),
            pltpu.SemaphoreType.DMA((40,)),
        ],
        compiler_params=pltpu.CompilerParams(
            collective_id=0, has_side_effects=True, vmem_limit_bytes=52 * 1024 * 1024
        ),
    )(normed, wz, gamma, curv_root, directions)


def per_device(
    images, dw_weight, dw_bias, ln_gain, ln_bias, w_in, b_in, gamma, curv_root, directions
):
    normed = features(images, dw_weight, dw_bias, ln_gain, ln_bias)
    normed = jnp.pad(normed, ((0, 0), (0, 0), (0, PAD - SIDE), (0, 0))).reshape(ROWS, CH)
    weights = w_in.T.reshape(UNITS, 2, 512).transpose(1, 0, 2).reshape(16, 512)
    bias = jnp.broadcast_to(b_in[None, :, None], (2, UNITS, 128)).reshape(16, 128)
    wz = jnp.concatenate([weights, bias], axis=1)
    out = step(normed, wz, gamma.reshape(1, OUTC), curv_root, directions.reshape(UNITS, OUTC))
    return out.reshape(UNITS, 1, OUTC)


def solution(mesh):
    placed = (
        P(("wide", "narrow"), None, None, None),
        P(),
        P(),
        P(),
        P(),
        P(None, ("wide", "narrow")),
        P(("wide", "narrow")),
        P(),
        P(("wide", "narrow"), None, None, None),
        P(("wide", "narrow"), None, None),
    )
    return jax.shard_map(
        per_device,
        mesh=mesh,
        in_specs=placed,
        out_specs=P(("wide", "narrow"), None, None),
        check_vma=False,
    )
```

```python
import jax
import jax.numpy as jnp
from jax import lax
from jax.experimental import pallas as pl
from jax.experimental.pallas import tpu as pltpu
from jax.sharding import PartitionSpec as P

damping = 0.05
scale_coef = 0.4
clip_ratio = 1.2

MESH = pl.DeviceIdType.MESH
F32 = jnp.float32
BF16 = jnp.bfloat16

CH = 1024
HID = 2048
OUTC = 512
SIDE = 14
KER = 7
IMGS = 4
CELLS = SIDE * SIDE
ROWS = IMGS * CELLS
ALL_CELLS = 1024 * CELLS
UNITS = 8
BLOCK = 64
WROWS = 8 * BLOCK + 16
DROWS = 4 * BLOCK
TILE = 256
PAIR = 2 * SIDE


def gelu(pre):
    return 0.5 * pre * (1.0 + lax.erf(pre * 0.7071067811865476))


def low_rows(shape):
    return lax.broadcasted_iota(jnp.int32, shape, len(shape) - 2) < 4


def folded(values):
    return values + pltpu.roll(values, 4, values.ndim - 2)


def unzip(values):
    count = values.shape[0] // 2
    pairs = values.reshape(count, 2, 8, 128)
    even, odd = pairs[:, 0], pairs[:, 1]
    low = low_rows((count, 8, 128))
    return (
        jnp.where(low, even, pltpu.roll(odd, 4, 1)),
        jnp.where(low, pltpu.roll(even, 4, 1), odd),
    )


def body(
    images_hbm,
    kernel_hbm,
    dw_bias_ref,
    gain_ref,
    ln_bias_ref,
    w_ref,
    b_ref,
    gamma_ref,
    curv_hbm,
    dir_ref,
    out_ref,
    images,
    kernel,
    roots,
    pixels,
    taps,
    scales,
    mixed,
    normed,
    curvature,
    wz,
    dz,
    wbuf,
    dbuf,
    hidden,
    cell_out,
    cell_weight,
    pair_send,
    pair_recv,
    slab_send,
    slab_recv,
    block_send,
    block_recv,
    row_send,
    row_recv,
    sums,
    sums_recv,
    wide_sums,
    wide_recv,
    send,
    recv,
    load,
):
    loads = [
        pltpu.make_async_copy(images_hbm, images, load.at[0]),
        pltpu.make_async_copy(kernel_hbm, kernel, load.at[1]),
        pltpu.make_async_copy(curv_hbm, roots, load.at[2]),
    ]
    for copy in loads:
        copy.start()

    wide = lax.axis_index("wide")
    narrow = lax.axis_index("narrow")
    x = wide // 16
    z = (wide // 2) % 8
    y = (wide % 2) * 2 + narrow // 2
    c = narrow % 2
    a3 = x + c * (y - x)
    a2 = y + c * (x - y)

    def at(x_, y_, z_, c_):
        return ((x_ * 8 + z_) * 2 + y_ // 2, (y_ % 2) * 2 + c_)

    def along(k3, k2, kz):
        a3_ = (a3 + k3) % 4
        a2_ = (a2 + k2) % 4
        return at(a3_ + c * (a2_ - a3_), a2_ + c * (a3_ - a2_), (z + kz) % 8, c)

    sibling = at(x, y, z, 1 - c)

    def group_of(k):
        spot = (z * 2 + c + k) % 16
        return at(x, y, spot // 2, spot % 2)

    def plane_of(k):
        spot = (x * 4 + y + k) % 16
        return at(spot // 4, spot % 4, z, c)

    def remote(src, dst, sem, device):
        return pltpu.make_async_remote_copy(
            src_ref=src,
            dst_ref=dst,
            send_sem=send.at[sem],
            recv_sem=recv.at[sem],
            device_id=device,
            device_id_type=MESH,
        )

    def arrived(sem, ref):
        pltpu.make_async_copy(ref, ref, recv.at[sem]).wait()

    def left(sem, ref):
        pltpu.make_async_copy(ref, ref, send.at[sem]).wait()

    barrier = pltpu.get_barrier_semaphore()
    for k in range(1, 16):
        pl.semaphore_signal(barrier, inc=1, device_id=group_of(k), device_id_type=MESH)
        pl.semaphore_signal(barrier, inc=1, device_id=plane_of(k), device_id_type=MESH)

    wz[0, :, 0:512] = w_ref[...]
    row8 = lax.broadcasted_iota(jnp.int32, (8, 8), 0)
    lane8 = lax.broadcasted_iota(jnp.int32, (8, 8), 1)
    line = jnp.broadcast_to(b_ref[...].astype(F32), (8, 8))
    column = jnp.sum(jnp.where(row8 == lane8, line, 0.0), axis=1, keepdims=True)
    column = jnp.broadcast_to(column, (8, 128))
    wz[0, :, 512:640] = jnp.concatenate([column, column], axis=0).astype(BF16)
    own = dir_ref[...]
    dz[0] = jnp.concatenate([own[:, :256], own[:, 256:]], axis=0).astype(BF16)

    def gather_z(buf, sem):
        for k in range(1, 8):
            remote(buf.at[0], buf.at[8 - k], sem, along(0, 0, k)).start()

    def gather_a2(buf, sem):
        for k in range(1, 4):
            remote(buf.at[0, 0, 0], buf.at[0, 0, 4 - k], sem, along(0, k, 0)).start()

    def spread(buf, k, lo, count, sem):
        part = pl.ds(lo, count)
        remote(buf.at[0, 0, part], buf.at[0, 4 - k, part], sem, along(k, 0, 0)).start()

    def to_sibling(buf, off, sem):
        remote(buf.at[0, off], buf.at[1, off], sem, sibling).start()

    def unpack_w():
        raw = wz[...].astype(F32)
        halves = (raw[:, :8, :512].reshape(BLOCK, 512), raw[:, 8:, :512].reshape(BLOCK, 512))
        for k in range(8):
            piece = halves[k // 4][:, (k % 4) * 128 : (k % 4 + 1) * 128]
            wbuf[0, 0, 0, k * BLOCK : (k + 1) * BLOCK, :] = piece.astype(BF16)
        bias = raw[:, :8, 512:].reshape(BLOCK, 128)
        row_at = lax.broadcasted_iota(jnp.int32, (BLOCK, 128), 0)
        lane_at = lax.broadcasted_iota(jnp.int32, (BLOCK, 128), 1) % BLOCK
        total = jnp.sum(jnp.where(row_at == lane_at, bias, 0.0), axis=0, keepdims=True)
        wbuf[0, 0, 0, 8 * BLOCK :, :] = jnp.broadcast_to(total, (16, 128)).astype(BF16)

    def unpack_d():
        raw = dz[...].astype(F32)
        halves = (raw[:, :8].reshape(BLOCK, 256), raw[:, 8:].reshape(BLOCK, 256))
        for k in range(4):
            piece = halves[k // 2][:, (k % 2) * 128 : (k % 2 + 1) * 128]
            dbuf[0, 0, 0, k * BLOCK : (k + 1) * BLOCK, :] = piece.astype(BF16)

    def weight_tile(h, s):
        return jnp.concatenate(
            [wbuf[h, s, :, k * BLOCK : (k + 1) * BLOCK, :].reshape(TILE, 128) for k in range(8)], axis=1
        )

    def bias_tile(h, s):
        rows = wbuf[h, s, :, 8 * BLOCK :, :].astype(F32)
        lane = lax.broadcasted_iota(jnp.int32, (16, 128), 1)
        lines = [jnp.where(lane < BLOCK, rows[2 * k], rows[2 * k + 1])[:1] for k in range(2)]
        return jnp.concatenate(lines, axis=1)

    def direction_tile(h, s):
        return jnp.concatenate(
            [dbuf[h, s, :, k * BLOCK : (k + 1) * BLOCK, :].reshape(TILE, 128) for k in range(4)], axis=1
        )

    def two_tiles(row, j):
        return jnp.where(
            low_rows((8, 128)),
            jnp.broadcast_to(row[:, 2 * j * 128 : (2 * j + 1) * 128], (8, 128)),
            jnp.broadcast_to(row[:, (2 * j + 1) * 128 : (2 * j + 2) * 128], (8, 128)),
        )

    def conv_rows(first):
        @pl.loop(0, 4)
        def _(j):
            for r in (first, first + 1):
                acc = [None] * SIDE
                for kh in range(KER):
                    source = r + kh - KER // 2
                    if source < 0 or source >= SIDE:
                        continue
                    line = [taps[j, kh * KER + kw] for kw in range(KER)]
                    for col in range(SIDE):
                        value = pixels[j, source * SIDE + col]
                        for kw in range(KER):
                            to = col - kw + KER // 2
                            if 0 <= to < SIDE:
                                term = value * line[kw]
                                acc[to] = term if acc[to] is None else acc[to] + term
                shift = scales[0, j]
                for col in range(SIDE):
                    mixed[j, (r - first) * SIDE + col] = acc[col] + shift

    def norm_rows(first):
        parts = [mixed[j] for j in range(4)]
        total = jnp.sum(folded(parts[0] + parts[1] + parts[2] + parts[3]), axis=2, keepdims=True)
        average = total * (1.0 / CH)
        parts = [part - average for part in parts]
        squares = [part * part for part in parts]
        total = jnp.sum(folded(squares[0] + squares[1] + squares[2] + squares[3]), axis=2, keepdims=True)
        rstd = lax.rsqrt(total * (1.0 / CH) + 1e-06)
        lo = first * SIDE * IMGS
        for j in range(4):
            values = unzip(parts[j] * rstd * scales[1, j] + scales[2, j])
            for k in range(2):
                lane = (2 * j + k) * 128
                normed[lo : lo + PAIR * IMGS, lane : lane + 128] = (
                    values[k].reshape(PAIR * IMGS, 128).astype(BF16)
                )

    loads[1].wait()

    @pl.loop(0, KER)
    def _(kh):
        for kw in range(KER):
            line = kernel[kh, kw : kw + 1, :]
            for j in range(4):
                taps[j, kh * KER + kw] = two_tiles(line, j)

    for j in range(4):
        scales[0, j] = two_tiles(dw_bias_ref[...], j)
        scales[1, j] = two_tiles(gain_ref[...], j)
        scales[2, j] = two_tiles(ln_bias_ref[...], j)

    loads[0].wait()

    @pl.loop(0, SIDE)
    def _(r):
        cells = pl.ds(r * SIDE, SIDE)
        for j in range(2):
            block = images[cells, 16 * j : 16 * j + 16, :].astype(F32)
            pixels[2 * j, cells] = block[:, :8]
            pixels[2 * j + 1, cells] = block[:, 8:]

    W, D = 0, 20
    pl.semaphore_wait(barrier, 30)
    gather_z(wz, W)
    gather_z(dz, D)

    def conv(first):
        conv_rows(first)
        norm_rows(first)

    conv(0)
    conv(2)
    conv(4)

    arrived(W, wz.at[pl.ds(1, 7)])
    unpack_w()
    gather_a2(wbuf, W + 1)
    spread(wbuf, 1, 0, 1, W + 2)
    spread(wbuf, 3, 0, 1, W + 3)
    arrived(D, dz.at[pl.ds(1, 7)])
    unpack_d()
    gather_a2(dbuf, D + 1)

    conv(6)
    conv(8)

    arrived(W + 1, wbuf.at[0, 0, pl.ds(1, 3)])
    spread(wbuf, 1, 1, 3, W + 4)
    spread(wbuf, 3, 1, 3, W + 5)
    to_sibling(wbuf, 0, W + 6)

    conv(10)

    arrived(D + 1, dbuf.at[0, 0, pl.ds(1, 3)])
    to_sibling(dbuf, 0, D + 6)

    conv(12)

    for k in (1, 3, 2):
        spread(dbuf, k, 0, 4, D + 1 + k)

    def project(p, h, s):
        pre = lax.dot_general(
            normed[...], weight_tile(h, s), (((1,), (1,)), ((), ())), preferred_element_type=F32
        )
        hidden[:, p * TILE : (p + 1) * TILE] = gelu(pre + bias_tile(h, s)).astype(BF16)

    places = [(0, 0), (1, 0), (0, 3), (1, 3), (0, 1), (1, 1), (0, 2), (1, 2)]

    project(0, 0, 0)
    arrived(W + 6, wbuf.at[1, 0])
    project(1, 1, 0)

    loads[2].wait()
    for k in range(2):
        root = roots[:, 8 * k : 8 * k + 8, :]
        first, second = unzip(0.25 + root * root)
        curvature[2 * k] = first
        curvature[2 * k + 1] = second

    arrived(W + 2, wbuf.at[0, 3, pl.ds(0, 1)])
    arrived(W + 4, wbuf.at[0, 3, pl.ds(1, 3)])
    remote(wbuf.at[0, 3, pl.ds(0, 2)], wbuf.at[0, 2, pl.ds(0, 2)], W + 10, along(1, 0, 0)).start()
    to_sibling(wbuf, 3, W + 9)
    arrived(W + 3, wbuf.at[0, 1, pl.ds(0, 1)])
    arrived(W + 5, wbuf.at[0, 1, pl.ds(1, 3)])
    remote(wbuf.at[0, 1, pl.ds(2, 2)], wbuf.at[0, 2, pl.ds(2, 2)], W + 11, along(3, 0, 0)).start()
    to_sibling(wbuf, 1, W + 7)
    project(2, 0, 3)
    arrived(W + 9, wbuf.at[1, 3])
    project(3, 1, 3)
    project(4, 0, 1)
    arrived(W + 7, wbuf.at[1, 1])
    project(5, 1, 1)
    arrived(W + 10, wbuf.at[0, 2, pl.ds(0, 2)])
    arrived(W + 11, wbuf.at[0, 2, pl.ds(2, 2)])
    to_sibling(wbuf, 2, W + 8)
    project(6, 0, 2)
    for k in (1, 3, 2):
        arrived(D + 1 + k, dbuf.at[0, 4 - k])
        to_sibling(dbuf, 4 - k, D + 6 + 4 - k)
    arrived(W + 8, wbuf.at[1, 2])
    project(7, 1, 2)
    for off in range(4):
        arrived(D + 6 + off, dbuf.at[1, off])

    directions = jnp.concatenate([direction_tile(h, s) for h, s in places], axis=0)
    cell_out[...] = jnp.dot(hidden[...], directions, preferred_element_type=F32)

    scale = gamma_ref[...] * gamma_ref[...]
    for k in range(4):
        lanes = slice(k * 128, (k + 1) * 128)
        values = cell_out[:, lanes].reshape(CELLS // 2, 8, 128)
        mean = folded(jnp.sum(values, axis=0)) * (1.0 / CELLS)
        inner = curvature[k] * (values - mean)
        again = folded(jnp.sum(inner, axis=0)) * (1.0 / CELLS)
        final = (inner - again) * scale[:, lanes]
        cell_weight[:, lanes] = final.reshape(ROWS, 128).astype(BF16)

    def product(h, s):
        p = places.index((h, s))
        return lax.dot_general(
            hidden[:, p * TILE : (p + 1) * TILE],
            cell_weight[...],
            (((0,), (0,)), ((), ())),
            preferred_element_type=F32,
        )

    R = 40
    for off in (2, 1, 3, 0):
        pair_send[off] = product(1, off).astype(BF16)
        remote(pair_send.at[off], pair_recv.at[off], R + off, sibling).start()
    for off in (2, 1, 3):
        part = product(0, off)
        arrived(R + off, pair_recv.at[off])
        slab_send[off - 1] = (part + pair_recv[off].astype(F32)).astype(BF16)
        remote(slab_send.at[off - 1], slab_recv.at[off - 1], R + 3 + off, along(off, 0, 0)).start()
    part = product(0, 0)
    arrived(R, pair_recv.at[0])
    part = part + pair_recv[0].astype(F32)
    for off in (1, 3, 2):
        arrived(R + 3 + off, slab_recv.at[off - 1])
        part = part + slab_recv[off - 1].astype(F32)
    blocks = part.reshape(4, BLOCK, OUTC)
    for off in (2, 1, 3):
        block_send[off - 1] = blocks[off].astype(BF16)
        remote(block_send.at[off - 1], block_recv.at[off - 1], R + 6 + off, along(0, off, 0)).start()
    part = blocks[0]
    for off in (1, 3, 2):
        arrived(R + 6 + off, block_recv.at[off - 1])
        part = part + block_recv[off - 1].astype(F32)
    rows = part.reshape(8, UNITS, OUTC)
    for k in (4, 3, 5, 2, 6, 1, 7):
        row_send[k - 1] = jnp.concatenate([rows[k, :, :256], rows[k, :, 256:]], axis=0).astype(BF16)
        remote(row_send.at[k - 1], row_recv.at[k - 1], R + 10, along(0, 0, k)).start()
    arrived(R + 10, row_recv)
    others = jnp.sum(row_recv[...].astype(F32), axis=0)
    summed = rows[0] + jnp.concatenate([others[:8], others[8:]], axis=1)

    estimate = dir_ref[...]
    fresh = estimate + (1.0 - damping) * estimate - summed * (1.0 / (scale_coef * ALL_CELLS))
    fresh_part = jnp.sum(fresh * fresh, axis=(0, 1), keepdims=True)
    direction_part = jnp.sum(estimate * estimate, axis=(0, 1), keepdims=True)
    row = lax.broadcasted_iota(jnp.int32, (8, 128), 0)
    sums[...] = jnp.where(row < 4, fresh_part, direction_part)
    for k in range(1, 16):
        remote(sums, sums_recv.at[k - 1], R + 11, group_of(k)).start()
    arrived(R + 11, sums_recv)
    wide_sums[...] = sums[...] + jnp.sum(sums_recv[...], axis=0)
    for k in range(1, 16):
        remote(wide_sums, wide_recv.at[k - 1], R + 12, plane_of(k)).start()
    arrived(R + 12, wide_recv)
    sq = wide_sums[...] + jnp.sum(wide_recv[...], axis=0)
    fresh_sq = sq[0:1, 0:1]
    direction_sq = sq[4:5, 0:1]
    factor = jnp.minimum(1.0, clip_ratio * jnp.sqrt(direction_sq / (fresh_sq + 1e-06)))
    out_ref[...] = fresh * factor

    for buf, zbuf, base in ((wbuf, wz, W), (dbuf, dz, D)):
        left(base, zbuf.at[pl.ds(1, 7)])
        left(base + 1, buf.at[0, 0, pl.ds(1, 3)])
        for off in range(4):
            left(base + 6 + off, buf.at[0, off])
    for k in range(2):
        left(W + 2 + k, wbuf.at[0, 0, pl.ds(0, 1)])
        left(W + 4 + k, wbuf.at[0, 0, pl.ds(1, 3)])
        left(W + 10 + k, wbuf.at[0, 0, pl.ds(0, 2)])
    for k in (1, 3, 2):
        left(D + 1 + k, dbuf.at[0, 0])
    for off in range(4):
        left(R + off, pair_send.at[off])
    for off in range(1, 4):
        left(R + 3 + off, slab_send.at[off - 1])
        left(R + 6 + off, block_send.at[off - 1])
    left(R + 10, row_recv)
    left(R + 11, sums_recv)
    left(R + 12, wide_recv)


def step(*operands):
    vmem = pl.BlockSpec(memory_space=pltpu.VMEM)
    hbm = pl.BlockSpec(memory_space=pl.ANY)
    return pl.pallas_call(
        body,
        out_shape=jax.ShapeDtypeStruct((UNITS, OUTC), F32),
        in_specs=[hbm, hbm, vmem, vmem, vmem, vmem, vmem, vmem, hbm, vmem],
        out_specs=vmem,
        scratch_shapes=[
            pltpu.VMEM((CELLS, 32, 128), BF16),
            pltpu.VMEM((KER, KER, CH), F32),
            pltpu.VMEM((CELLS, 16, 128), F32),
            pltpu.VMEM((4, CELLS, 8, 128), F32),
            pltpu.VMEM((4, KER * KER, 8, 128), F32),
            pltpu.VMEM((3, 4, 8, 128), F32),
            pltpu.VMEM((4, PAIR, 8, 128), F32),
            pltpu.VMEM((ROWS, CH), BF16),
            pltpu.VMEM((4, CELLS // 2, 8, 128), F32),
            pltpu.VMEM((8, 16, 640), BF16),
            pltpu.VMEM((8, 16, 256), BF16),
            pltpu.VMEM((2, 4, 4, WROWS, 128), BF16),
            pltpu.VMEM((2, 4, 4, DROWS, 128), BF16),
            pltpu.VMEM((ROWS, HID), BF16),
            pltpu.VMEM((ROWS, OUTC), F32),
            pltpu.VMEM((ROWS, OUTC), BF16),
            pltpu.VMEM((4, TILE, OUTC), BF16),
            pltpu.VMEM((4, TILE, OUTC), BF16),
            pltpu.VMEM((3, TILE, OUTC), BF16),
            pltpu.VMEM((3, TILE, OUTC), BF16),
            pltpu.VMEM((3, BLOCK, OUTC), BF16),
            pltpu.VMEM((3, BLOCK, OUTC), BF16),
            pltpu.VMEM((7, 16, 256), BF16),
            pltpu.VMEM((7, 16, 256), BF16),
            pltpu.VMEM((8, 128), F32),
            pltpu.VMEM((15, 8, 128), F32),
            pltpu.VMEM((8, 128), F32),
            pltpu.VMEM((15, 8, 128), F32),
            pltpu.SemaphoreType.DMA((60,)),
            pltpu.SemaphoreType.DMA((60,)),
            pltpu.SemaphoreType.DMA((3,)),
        ],
        compiler_params=pltpu.CompilerParams(
            collective_id=0, has_side_effects=True, vmem_limit_bytes=56 * 1024 * 1024
        ),
    )(*operands)


def cell_major(array):
    tiles = array.shape[3] // 128
    cells = array.transpose(1, 2, 0, 3).reshape(CELLS, IMGS, tiles, 128)
    return cells.transpose(0, 2, 1, 3).reshape(CELLS, tiles * IMGS, 128)


def per_device(
    images, dw_weight, dw_bias, ln_gain, ln_bias, w_in, b_in, gamma, curv_root, directions
):
    out = step(
        cell_major(images),
        dw_weight,
        dw_bias.reshape(1, CH),
        ln_gain.reshape(1, CH),
        ln_bias.reshape(1, CH),
        w_in.T.reshape(UNITS, 2, 512).transpose(1, 0, 2).reshape(16, 512),
        b_in.reshape(1, UNITS),
        gamma.reshape(1, OUTC),
        cell_major(curv_root),
        directions.reshape(UNITS, OUTC),
    )
    return out.reshape(UNITS, 1, OUTC)


def solution(mesh):
    placed = (
        P(("wide", "narrow"), None, None, None),
        P(),
        P(),
        P(),
        P(),
        P(None, ("wide", "narrow")),
        P(("wide", "narrow")),
        P(),
        P(("wide", "narrow"), None, None, None),
        P(("wide", "narrow"), None, None),
    )
    return jax.shard_map(
        per_device,
        mesh=mesh,
        in_specs=placed,
        out_specs=P(("wide", "narrow"), None, None),
        check_vma=False,
    )
```

```python
import jax
import jax.numpy as jnp
from jax import lax
from jax.experimental import pallas as pl
from jax.experimental.pallas import tpu as pltpu
from jax.sharding import PartitionSpec as P

damping = 0.05
scale_coef = 0.4
clip_ratio = 1.2

MESH = pl.DeviceIdType.MESH
F32 = jnp.float32
BF16 = jnp.bfloat16

CH = 1024
HID = 2048
OUTC = 512
SIDE = 14
KER = 7
IMGS = 4
CELLS = SIDE * SIDE
ROWS = IMGS * CELLS
ALL_CELLS = 1024 * CELLS
UNITS = 8
BLOCK = 64
CROWS = 4 * BLOCK
TILE = 256
PAIR = 2 * SIDE


def gelu(pre):
    return 0.5 * pre * (1.0 + lax.erf(pre * 0.7071067811865476))


def low_rows(shape):
    return lax.broadcasted_iota(jnp.int32, shape, len(shape) - 2) < 4


def folded(values):
    return values + pltpu.roll(values, 4, values.ndim - 2)


def unzip(values):
    count = values.shape[0] // 2
    pairs = values.reshape(count, 2, 8, 128)
    even, odd = pairs[:, 0], pairs[:, 1]
    low = low_rows((count, 8, 128))
    return (
        jnp.where(low, even, pltpu.roll(odd, 4, 1)),
        jnp.where(low, pltpu.roll(even, 4, 1), odd),
    )


def body(
    images_hbm,
    kernel_hbm,
    dw_bias_ref,
    gain_ref,
    ln_bias_ref,
    w_ref,
    b_ref,
    gamma_ref,
    curv_hbm,
    dir_ref,
    out_ref,
    images,
    kernel,
    roots,
    pixels,
    taps,
    scales,
    mixed,
    normed,
    curvature,
    z_low,
    z_high,
    z_dir,
    w_low,
    w_high,
    w_dir,
    late,
    hidden,
    cell_out,
    cell_weight,
    pair_send,
    pair_recv,
    slab_send,
    slab_recv,
    kept,
    block_send,
    block_recv,
    row_send,
    row_recv,
    sums,
    sums_recv,
    wide_sums,
    wide_recv,
    send,
    recv,
    load,
):
    loads = [
        pltpu.make_async_copy(images_hbm, images, load.at[0]),
        pltpu.make_async_copy(kernel_hbm, kernel, load.at[1]),
        pltpu.make_async_copy(curv_hbm, roots, load.at[2]),
    ]
    for copy in loads:
        copy.start()

    wide = lax.axis_index("wide")
    narrow = lax.axis_index("narrow")
    x = wide // 16
    z = (wide // 2) % 8
    y = (wide % 2) * 2 + narrow // 2
    c = narrow % 2
    a3 = x + c * (y - x)
    a2 = y + c * (x - y)

    def at(x_, y_, z_, c_):
        return ((x_ * 8 + z_) * 2 + y_ // 2, (y_ % 2) * 2 + c_)

    def along(k3, k2, kz):
        a3_ = (a3 + k3) % 4
        a2_ = (a2 + k2) % 4
        return at(a3_ + c * (a2_ - a3_), a2_ + c * (a3_ - a2_), (z + kz) % 8, c)

    sibling = at(x, y, z, 1 - c)

    def group_of(k):
        spot = (z * 2 + c + k) % 16
        return at(x, y, spot // 2, spot % 2)

    def plane_of(k):
        spot = (x * 4 + y + k) % 16
        return at(spot // 4, spot % 4, z, c)

    def remote(src, dst, sem, device):
        return pltpu.make_async_remote_copy(
            src_ref=src,
            dst_ref=dst,
            send_sem=send.at[sem],
            recv_sem=recv.at[sem],
            device_id=device,
            device_id_type=MESH,
        )

    def arrived(sem, ref):
        pltpu.make_async_copy(ref, ref, recv.at[sem]).wait()

    def left(sem, ref):
        pltpu.make_async_copy(ref, ref, send.at[sem]).wait()

    barrier = pltpu.get_barrier_semaphore()
    for k in range(1, 16):
        pl.semaphore_signal(barrier, inc=1, device_id=group_of(k), device_id_type=MESH)
        pl.semaphore_signal(barrier, inc=1, device_id=plane_of(k), device_id_type=MESH)

    z_low[0] = w_ref[0:16, :]
    z_high[0, :, 0:256] = w_ref[16:32, :]
    row8 = lax.broadcasted_iota(jnp.int32, (8, 8), 0)
    lane8 = lax.broadcasted_iota(jnp.int32, (8, 8), 1)
    line = jnp.broadcast_to(b_ref[...].astype(F32), (8, 8))
    column = jnp.sum(jnp.where(row8 == lane8, line, 0.0), axis=1, keepdims=True)
    column = jnp.broadcast_to(column, (8, 128))
    z_high[0, :, 256:384] = jnp.concatenate([column, column], axis=0).astype(BF16)
    own = dir_ref[:, 0, :]
    z_dir[0] = jnp.concatenate([own[:, :128], own[:, 128:256]], axis=0).astype(BF16)
    late[0, 0, 0, 0] = jnp.concatenate([own[:, 256:384], own[:, 384:]], axis=0).astype(BF16)

    def gather_z(buf, sem):
        for k in range(1, 8):
            remote(buf.at[0], buf.at[8 - k], sem, along(0, 0, k)).start()

    def gather_a2(buf, sem):
        for k in range(1, 4):
            remote(buf.at[0, 0, 0], buf.at[0, 0, 4 - k], sem, along(0, k, 0)).start()

    def spread(buf, k, lo, count, sem):
        part = pl.ds(lo, count)
        remote(buf.at[0, 0, part], buf.at[0, 4 - k, part], sem, along(k, 0, 0)).start()

    def to_sibling(buf, off, sem):
        remote(buf.at[0, off], buf.at[1, off], sem, sibling).start()

    def unpack(zbuf, buf):
        raw = zbuf[...].astype(F32)
        tiles = zbuf.shape[2] // 256 * 4 or 2
        width = tiles * 64
        halves = (raw[:, :8, :width].reshape(BLOCK, width), raw[:, 8:, :width].reshape(BLOCK, width))
        for k in range(tiles):
            lane = k * 128 % width
            piece = halves[k // (tiles // 2)][:, lane : lane + 128]
            buf[0, 0, 0, k * BLOCK : (k + 1) * BLOCK, :] = piece.astype(BF16)
        if zbuf.shape[2] > 256:
            bias = raw[:, :8, 256:].reshape(BLOCK, 128)
            row_at = lax.broadcasted_iota(jnp.int32, (BLOCK, 128), 0)
            lane_at = lax.broadcasted_iota(jnp.int32, (BLOCK, 128), 1) % BLOCK
            total = jnp.sum(jnp.where(row_at == lane_at, bias, 0.0), axis=0, keepdims=True)
            buf[0, 0, 0, CROWS:, :] = jnp.broadcast_to(total, (16, 128)).astype(BF16)

    def chunk_tile(buf, h, s, tiles=4):
        return jnp.concatenate(
            [buf[h, s, :, k * BLOCK : (k + 1) * BLOCK, :].reshape(TILE, 128) for k in range(tiles)], axis=1
        )

    def late_tile(h, s):
        raw = late[h, :, s].astype(F32)
        sides = [
            jnp.concatenate([raw[kz, k2, lo : lo + 8] for k2 in range(4) for kz in range(8)], axis=0)
            for lo in (0, 8)
        ]
        return jnp.concatenate(sides, axis=1).astype(BF16)

    def bias_tile(h, s):
        rows = w_high[h, s, :, CROWS:, :].astype(F32)
        lane = lax.broadcasted_iota(jnp.int32, (16, 128), 1)
        lines = [jnp.where(lane < BLOCK, rows[2 * k], rows[2 * k + 1])[:1] for k in range(2)]
        return jnp.concatenate(lines, axis=1)

    def two_tiles(row, j):
        return jnp.where(
            low_rows((8, 128)),
            jnp.broadcast_to(row[:, 2 * j * 128 : (2 * j + 1) * 128], (8, 128)),
            jnp.broadcast_to(row[:, (2 * j + 1) * 128 : (2 * j + 2) * 128], (8, 128)),
        )

    def conv_rows(first):
        @pl.loop(0, 4)
        def _(j):
            for r in (first, first + 1):
                acc = [None] * SIDE
                for kh in range(KER):
                    source = r + kh - KER // 2
                    if source < 0 or source >= SIDE:
                        continue
                    line = [taps[j, kh * KER + kw] for kw in range(KER)]
                    for col in range(SIDE):
                        value = pixels[j, source * SIDE + col]
                        for kw in range(KER):
                            to = col - kw + KER // 2
                            if 0 <= to < SIDE:
                                term = value * line[kw]
                                acc[to] = term if acc[to] is None else acc[to] + term
                shift = scales[0, j]
                for col in range(SIDE):
                    mixed[j, (r - first) * SIDE + col] = acc[col] + shift

    def norm_rows(first):
        parts = [mixed[j] for j in range(4)]
        total = jnp.sum(folded(parts[0] + parts[1] + parts[2] + parts[3]), axis=2, keepdims=True)
        average = total * (1.0 / CH)
        parts = [part - average for part in parts]
        squares = [part * part for part in parts]
        total = jnp.sum(folded(squares[0] + squares[1] + squares[2] + squares[3]), axis=2, keepdims=True)
        rstd = lax.rsqrt(total * (1.0 / CH) + 1e-06)
        lo = first * SIDE * IMGS
        for j in range(4):
            values = unzip(parts[j] * rstd * scales[1, j] + scales[2, j])
            for k in range(2):
                lane = (2 * j + k) * 128
                normed[lo : lo + PAIR * IMGS, lane : lane + 128] = (
                    values[k].reshape(PAIR * IMGS, 128).astype(BF16)
                )

    loads[1].wait()

    @pl.loop(0, KER)
    def _(kh):
        for kw in range(KER):
            line = kernel[kh, kw : kw + 1, :]
            for j in range(4):
                taps[j, kh * KER + kw] = two_tiles(line, j)

    for j in range(4):
        scales[0, j] = two_tiles(dw_bias_ref[...], j)
        scales[1, j] = two_tiles(gain_ref[...], j)
        scales[2, j] = two_tiles(ln_bias_ref[...], j)

    loads[0].wait()

    @pl.loop(0, SIDE)
    def _(r):
        cells = pl.ds(r * SIDE, SIDE)
        for j in range(2):
            block = images[cells, 16 * j : 16 * j + 16, :].astype(F32)
            pixels[2 * j, cells] = block[:, :8]
            pixels[2 * j + 1, cells] = block[:, 8:]

    chunks = ((z_low, w_low, 0), (z_high, w_high, 20), (z_dir, w_dir, 40))
    LOW, HIGH, DIR = chunks

    def conv(first):
        conv_rows(first)
        norm_rows(first)

    def after_z(chunk):
        zbuf, buf, sem = chunk
        arrived(sem, zbuf.at[pl.ds(1, 7)])
        unpack(zbuf, buf)
        gather_a2(buf, sem + 1)
        if chunk is not DIR:
            spread(buf, 1, 0, 1, sem + 2)
            spread(buf, 3, 0, 1, sem + 3)

    def after_a2(chunk):
        _, buf, sem = chunk
        arrived(sem + 1, buf.at[0, 0, pl.ds(1, 3)])
        if chunk is DIR:
            for k in (1, 3, 2):
                spread(buf, k, 0, 4, sem + 1 + k)
        else:
            spread(buf, 1, 1, 3, sem + 4)
            spread(buf, 3, 1, 3, sem + 5)
        to_sibling(buf, 0, sem + 6)

    def after_a3(chunk):
        _, buf, sem = chunk
        arrived(sem + 2, buf.at[0, 3, pl.ds(0, 1)])
        arrived(sem + 4, buf.at[0, 3, pl.ds(1, 3)])
        remote(buf.at[0, 3, pl.ds(0, 2)], buf.at[0, 2, pl.ds(0, 2)], sem + 10, along(1, 0, 0)).start()
        arrived(sem + 3, buf.at[0, 1, pl.ds(0, 1)])
        arrived(sem + 5, buf.at[0, 1, pl.ds(1, 3)])
        remote(buf.at[0, 1, pl.ds(2, 2)], buf.at[0, 2, pl.ds(2, 2)], sem + 11, along(3, 0, 0)).start()
        to_sibling(buf, 3, sem + 9)
        to_sibling(buf, 1, sem + 7)

    def after_forward(chunk):
        _, buf, sem = chunk
        arrived(sem + 10, buf.at[0, 2, pl.ds(0, 2)])
        arrived(sem + 11, buf.at[0, 2, pl.ds(2, 2)])
        to_sibling(buf, 2, sem + 8)

    def from_sibling(chunk, off):
        _, buf, sem = chunk
        arrived(sem + 6 + off, buf.at[1, off])

    def project(p, h, s):
        weights = jnp.concatenate([chunk_tile(w_low, h, s), chunk_tile(w_high, h, s)], axis=1)
        pre = lax.dot_general(
            normed[...], weights, (((1,), (1,)), ((), ())), preferred_element_type=F32
        )
        hidden[:, p * TILE : (p + 1) * TILE] = gelu(pre + bias_tile(h, s)).astype(BF16)

    places = [(0, 0), (1, 0), (0, 3), (1, 3), (0, 1), (1, 1), (0, 2), (1, 2)]

    pl.semaphore_wait(barrier, 30)
    L = 60
    for k in range(1, 4):
        remote(late.at[0, 0, 0, 0], late.at[0, 0, 0, 4 - k], L, along(0, k, 0)).start()
    for zbuf, _, sem in chunks:
        gather_z(zbuf, sem)

    conv(0)
    conv(2)
    arrived(L, late.at[0, 0, 0, pl.ds(1, 3)])
    for k in range(1, 4):
        remote(late.at[0, 0, 0], late.at[0, 0, 4 - k], L + 1, along(k, 0, 0)).start()
    conv(4)
    after_z(LOW)
    after_z(HIGH)
    arrived(L + 1, late.at[0, 0, pl.ds(1, 3)])
    for k in (4, 3, 5, 2, 6, 1, 7):
        remote(late.at[0, 0], late.at[0, 8 - k], L + 2, along(0, 0, k)).start()
    conv(6)
    after_z(DIR)
    conv(8)
    after_a2(LOW)
    conv(10)
    after_a2(HIGH)
    conv(12)
    after_a2(DIR)

    loads[2].wait()
    for k in range(2):
        root = roots[:, 8 * k : 8 * k + 8, :]
        first, second = unzip(0.25 + root * root)
        curvature[2 * k] = first
        curvature[2 * k + 1] = second

    project(0, 0, 0)
    after_a3(LOW)
    from_sibling(LOW, 0)
    from_sibling(HIGH, 0)
    project(1, 1, 0)
    after_a3(HIGH)
    project(2, 0, 3)
    project(4, 0, 1)
    arrived(L + 2, late.at[0, pl.ds(1, 7)])
    remote(late.at[0], late.at[1], L + 3, sibling).start()
    for k in (1, 3, 2):
        arrived(40 + 1 + k, w_dir.at[0, 4 - k])
        to_sibling(w_dir, 4 - k, 40 + 6 + 4 - k)
    after_forward(LOW)
    for off in (3, 1):
        from_sibling(LOW, off)
        from_sibling(HIGH, off)
    project(3, 1, 3)
    project(5, 1, 1)

    def direction_tile(h, s):
        return jnp.concatenate([chunk_tile(w_dir, h, s, 2), late_tile(h, s)], axis=1)

    def partial(lo, hi):
        directions = jnp.concatenate([direction_tile(h, s) for h, s in places[lo:hi]], axis=0)
        return jnp.dot(hidden[:, lo * TILE : hi * TILE], directions, preferred_element_type=F32)

    after_forward(HIGH)
    for off in range(4):
        from_sibling(DIR, off)
    arrived(L + 3, late.at[1])
    cell_out[...] = partial(0, 6)
    project(6, 0, 2)
    from_sibling(LOW, 2)
    from_sibling(HIGH, 2)
    project(7, 1, 2)
    cell_out[...] += partial(6, 8)

    scale = gamma_ref[...] * gamma_ref[...]
    for k in range(4):
        lanes = slice(k * 128, (k + 1) * 128)
        values = cell_out[:, lanes].reshape(CELLS // 2, 8, 128)
        mean = folded(jnp.sum(values, axis=0)) * (1.0 / CELLS)
        inner = curvature[k] * (values - mean)
        again = folded(jnp.sum(inner, axis=0)) * (1.0 / CELLS)
        final = (inner - again) * scale[:, lanes]
        cell_weight[:, lanes] = final.reshape(ROWS, 128).astype(BF16)

    def product(h, s):
        p = places.index((h, s))
        return lax.dot_general(
            hidden[:, p * TILE : (p + 1) * TILE],
            cell_weight[...],
            (((0,), (0,)), ((), ())),
            preferred_element_type=F32,
        )

    R = 64
    for off in (2, 1, 3, 0):
        pair_send[off] = product(1, off).astype(BF16)
        remote(pair_send.at[off], pair_recv.at[off], R + off, sibling).start()
    onward, home = pl.ds(1, 3), pl.ds(0, 1)
    for off in (2, 1, 3):
        part = product(0, off)
        arrived(R + off, pair_recv.at[off])
        part = part + pair_recv[off].astype(F32)
        slab_send[off - 1] = part.reshape(4, BLOCK, OUTC).astype(BF16)
        place = slab_recv.at[off - 1, onward]
        remote(slab_send.at[off - 1, onward], place, R + 3 + off, along(off, 0, 0)).start()
    for off in (2, 1, 3):
        place = slab_recv.at[off - 1, home]
        remote(slab_send.at[off - 1, home], place, R + 6 + off, along(off, 0, 0)).start()
    part = product(0, 0)
    arrived(R, pair_recv.at[0])
    kept[...] = (part + pair_recv[0].astype(F32)).reshape(4, BLOCK, OUTC)
    for off in (1, 3, 2):
        arrived(R + 3 + off, slab_recv.at[off - 1, onward])
    for k in (2, 1, 3):
        block = kept[k]
        for off in (1, 2, 3):
            block = block + slab_recv[off - 1, k].astype(F32)
        block_send[k - 1] = block.astype(BF16)
        remote(block_send.at[k - 1], block_recv.at[k - 1], R + 9 + k, along(0, k, 0)).start()
    block = kept[0]
    for off in (1, 3, 2):
        arrived(R + 6 + off, slab_recv.at[off - 1, home])
        block = block + slab_recv[off - 1, 0].astype(F32)
    for off in (1, 3, 2):
        arrived(R + 9 + off, block_recv.at[off - 1])
        block = block + block_recv[off - 1].astype(F32)
    rows = block.reshape(8, UNITS, OUTC)
    for k in (4, 3, 5, 2, 6, 1, 7):
        row_send[k - 1] = jnp.concatenate([rows[k, :, :256], rows[k, :, 256:]], axis=0).astype(BF16)
        remote(row_send.at[k - 1], row_recv.at[k - 1], R + 13, along(0, 0, k)).start()
    arrived(R + 13, row_recv)
    others = jnp.sum(row_recv[...].astype(F32), axis=0)
    summed = rows[0] + jnp.concatenate([others[:8], others[8:]], axis=1)

    N = R + 14
    estimate = dir_ref[:, 0, :]
    fresh = estimate + (1.0 - damping) * estimate - summed * (1.0 / (scale_coef * ALL_CELLS))
    fresh_part = jnp.sum(fresh * fresh, axis=(0, 1), keepdims=True)
    direction_part = jnp.sum(estimate * estimate, axis=(0, 1), keepdims=True)
    row = lax.broadcasted_iota(jnp.int32, (8, 128), 0)
    sums[...] = jnp.where(row < 4, fresh_part, direction_part)
    for k in range(1, 16):
        remote(sums, sums_recv.at[k - 1], N, group_of(k)).start()
    arrived(N, sums_recv)
    wide_sums[...] = sums[...] + jnp.sum(sums_recv[...], axis=0)
    for k in range(1, 16):
        remote(wide_sums, wide_recv.at[k - 1], N + 1, plane_of(k)).start()
    arrived(N + 1, wide_recv)
    sq = wide_sums[...] + jnp.sum(wide_recv[...], axis=0)
    fresh_sq = sq[0:1, 0:1]
    direction_sq = sq[4:5, 0:1]
    factor = jnp.minimum(1.0, clip_ratio * jnp.sqrt(direction_sq / (fresh_sq + 1e-06)))
    out_ref[...] = fresh * factor

    for zbuf, buf, base in chunks:
        left(base, zbuf.at[pl.ds(1, 7)])
        left(base + 1, buf.at[0, 0, pl.ds(1, 3)])
        for off in range(4):
            left(base + 6 + off, buf.at[0, off])
    for _, buf, base in (LOW, HIGH):
        for k in range(2):
            left(base + 2 + k, buf.at[0, 0, pl.ds(0, 1)])
            left(base + 4 + k, buf.at[0, 0, pl.ds(1, 3)])
            left(base + 10 + k, buf.at[0, 0, pl.ds(0, 2)])
    for k in (1, 3, 2):
        left(40 + 1 + k, w_dir.at[0, 0])
    left(L, late.at[0, 0, 0, pl.ds(1, 3)])
    left(L + 1, late.at[0, 0, pl.ds(1, 3)])
    left(L + 2, late.at[0, pl.ds(1, 7)])
    left(L + 3, late.at[0])
    for off in range(4):
        left(R + off, pair_send.at[off])
    for off in range(1, 4):
        left(R + 3 + off, slab_send.at[off - 1, onward])
        left(R + 6 + off, slab_send.at[off - 1, home])
        left(R + 9 + off, block_send.at[off - 1])
    left(R + 13, row_recv)
    left(N, sums_recv)
    left(N + 1, wide_recv)


def step(*operands):
    vmem = pl.BlockSpec(memory_space=pltpu.VMEM)
    hbm = pl.BlockSpec(memory_space=pl.ANY)
    return pl.pallas_call(
        body,
        out_shape=jax.ShapeDtypeStruct((UNITS, OUTC), F32),
        in_specs=[hbm, hbm, vmem, vmem, vmem, vmem, vmem, vmem, hbm, vmem],
        out_specs=vmem,
        scratch_shapes=[
            pltpu.VMEM((CELLS, 32, 128), BF16),
            pltpu.VMEM((KER, KER, CH), F32),
            pltpu.VMEM((CELLS, 16, 128), F32),
            pltpu.VMEM((4, CELLS, 8, 128), F32),
            pltpu.VMEM((4, KER * KER, 8, 128), F32),
            pltpu.VMEM((3, 4, 8, 128), F32),
            pltpu.VMEM((4, PAIR, 8, 128), F32),
            pltpu.VMEM((ROWS, CH), BF16),
            pltpu.VMEM((4, CELLS // 2, 8, 128), F32),
            pltpu.VMEM((8, 16, 256), BF16),
            pltpu.VMEM((8, 16, 384), BF16),
            pltpu.VMEM((8, 16, 128), BF16),
            pltpu.VMEM((2, 4, 4, CROWS, 128), BF16),
            pltpu.VMEM((2, 4, 4, CROWS + 16, 128), BF16),
            pltpu.VMEM((2, 4, 4, CROWS // 2, 128), BF16),
            pltpu.VMEM((2, 8, 4, 4, 16, 128), BF16),
            pltpu.VMEM((ROWS, HID), BF16),
            pltpu.VMEM((ROWS, OUTC), F32),
            pltpu.VMEM((ROWS, OUTC), BF16),
            pltpu.VMEM((4, TILE, OUTC), BF16),
            pltpu.VMEM((4, TILE, OUTC), BF16),
            pltpu.VMEM((3, 4, BLOCK, OUTC), BF16),
            pltpu.VMEM((3, 4, BLOCK, OUTC), BF16),
            pltpu.VMEM((4, BLOCK, OUTC), F32),
            pltpu.VMEM((3, BLOCK, OUTC), BF16),
            pltpu.VMEM((3, BLOCK, OUTC), BF16),
            pltpu.VMEM((7, 16, 256), BF16),
            pltpu.VMEM((7, 16, 256), BF16),
            pltpu.VMEM((8, 128), F32),
            pltpu.VMEM((15, 8, 128), F32),
            pltpu.VMEM((8, 128), F32),
            pltpu.VMEM((15, 8, 128), F32),
            pltpu.SemaphoreType.DMA((96,)),
            pltpu.SemaphoreType.DMA((96,)),
            pltpu.SemaphoreType.DMA((3,)),
        ],
        compiler_params=pltpu.CompilerParams(
            collective_id=0, has_side_effects=True, vmem_limit_bytes=56 * 1024 * 1024
        ),
    )(*operands)


def cell_major(array):
    tiles = array.shape[3] // 128
    cells = array.transpose(1, 2, 0, 3).reshape(CELLS, IMGS, tiles, 128)
    return cells.transpose(0, 2, 1, 3).reshape(CELLS, tiles * IMGS, 128)


def per_device(
    images, dw_weight, dw_bias, ln_gain, ln_bias, w_in, b_in, gamma, curv_root, directions
):
    out = step(
        cell_major(images),
        dw_weight,
        dw_bias.reshape(1, CH),
        ln_gain.reshape(1, CH),
        ln_bias.reshape(1, CH),
        w_in.T.reshape(UNITS, 4, 256).transpose(1, 0, 2).reshape(32, 256),
        b_in.reshape(1, UNITS),
        gamma.reshape(1, OUTC),
        cell_major(curv_root),
        directions,
    )
    return out.reshape(UNITS, 1, OUTC)


def solution(mesh):
    placed = (
        P(("wide", "narrow"), None, None, None),
        P(),
        P(),
        P(),
        P(),
        P(None, ("wide", "narrow")),
        P(("wide", "narrow")),
        P(),
        P(("wide", "narrow"), None, None, None),
        P(("wide", "narrow"), None, None),
    )
    return jax.shard_map(
        per_device,
        mesh=mesh,
        in_specs=placed,
        out_specs=P(("wide", "narrow"), None, None),
        check_vma=False,
    )
```

```python
import jax
import jax.numpy as jnp
from jax import lax
from jax.experimental import pallas as pl
from jax.experimental.pallas import tpu as pltpu
from jax.sharding import PartitionSpec as P

damping = 0.05
scale_coef = 0.4
clip_ratio = 1.2

MESH = pl.DeviceIdType.MESH
F32 = jnp.float32
BF16 = jnp.bfloat16

CH = 1024
HID = 2048
OUTC = 512
SIDE = 14
KER = 7
IMGS = 4
CELLS = SIDE * SIDE
ROWS = IMGS * CELLS
ALL_CELLS = 1024 * CELLS
UNITS = 8
BLOCK = 64
CROWS = 4 * BLOCK
TILE = 256
FAR_FIRST = (8, 7, 9, 6, 10, 5, 11, 4, 12, 3, 13, 2, 14, 1, 15)
PLANE_FAR_FIRST = (10, 9, 11, 6, 14, 5, 7, 13, 15, 2, 8, 1, 3, 4, 12)
PAIR = 2 * SIDE


def gelu(pre):
    return 0.5 * pre * (1.0 + lax.erf(pre * 0.7071067811865476))


def low_rows(shape):
    return lax.broadcasted_iota(jnp.int32, shape, len(shape) - 2) < 4


def folded(values):
    return values + pltpu.roll(values, 4, values.ndim - 2)


def unzip(values):
    count = values.shape[0] // 2
    pairs = values.reshape(count, 2, 8, 128)
    even, odd = pairs[:, 0], pairs[:, 1]
    low = low_rows((count, 8, 128))
    return (
        jnp.where(low, even, pltpu.roll(odd, 4, 1)),
        jnp.where(low, pltpu.roll(even, 4, 1), odd),
    )


def body(
    images_hbm,
    kernel_hbm,
    dw_bias_ref,
    gain_ref,
    ln_bias_ref,
    w_ref,
    b_ref,
    gamma_ref,
    curv_hbm,
    dir_ref,
    out_ref,
    images,
    kernel,
    roots,
    pixels,
    taps,
    scales,
    mixed,
    normed,
    curvature,
    z_low,
    z_high,
    z_dir,
    w_low,
    w_high,
    w_dir,
    late,
    hidden,
    cell_out,
    cell_weight,
    pair_send,
    pair_recv,
    slab_send,
    slab_recv,
    kept,
    block_send,
    block_recv,
    row_send,
    row_recv,
    sums,
    sums_recv,
    wide_sums,
    wide_recv,
    send,
    recv,
    load,
):
    loads = [
        pltpu.make_async_copy(images_hbm, images, load.at[0]),
        pltpu.make_async_copy(kernel_hbm, kernel, load.at[1]),
        pltpu.make_async_copy(curv_hbm, roots, load.at[2]),
    ]
    for copy in loads:
        copy.start()

    wide = lax.axis_index("wide")
    narrow = lax.axis_index("narrow")
    x = wide // 16
    z = (wide // 2) % 8
    y = (wide % 2) * 2 + narrow // 2
    c = narrow % 2
    a3 = x + c * (y - x)
    a2 = y + c * (x - y)

    def at(x_, y_, z_, c_):
        return ((x_ * 8 + z_) * 2 + y_ // 2, (y_ % 2) * 2 + c_)

    def along(k3, k2, kz):
        a3_ = (a3 + k3) % 4
        a2_ = (a2 + k2) % 4
        return at(a3_ + c * (a2_ - a3_), a2_ + c * (a3_ - a2_), (z + kz) % 8, c)

    sibling = at(x, y, z, 1 - c)

    def group_of(k):
        spot = (z * 2 + c + k) % 16
        return at(x, y, spot // 2, spot % 2)

    def plane_of(k):
        spot = (x * 4 + y + k) % 16
        return at(spot // 4, spot % 4, z, c)

    def remote(src, dst, sem, device):
        return pltpu.make_async_remote_copy(
            src_ref=src,
            dst_ref=dst,
            send_sem=send.at[sem],
            recv_sem=recv.at[sem],
            device_id=device,
            device_id_type=MESH,
        )

    def arrived(sem, ref):
        pltpu.make_async_copy(ref, ref, recv.at[sem]).wait()

    def left(sem, ref):
        pltpu.make_async_copy(ref, ref, send.at[sem]).wait()

    barrier = pltpu.get_barrier_semaphore()
    for k in FAR_FIRST:
        pl.semaphore_signal(barrier, inc=1, device_id=group_of(k), device_id_type=MESH)
        pl.semaphore_signal(barrier, inc=1, device_id=plane_of(k), device_id_type=MESH)

    z_low[0] = w_ref[0:16, :]
    z_high[0, :, 0:256] = w_ref[16:32, :]
    row8 = lax.broadcasted_iota(jnp.int32, (8, 8), 0)
    lane8 = lax.broadcasted_iota(jnp.int32, (8, 8), 1)
    line = jnp.broadcast_to(b_ref[...].astype(F32), (8, 8))
    column = jnp.sum(jnp.where(row8 == lane8, line, 0.0), axis=1, keepdims=True)
    column = jnp.broadcast_to(column, (8, 128))
    z_high[0, :, 256:384] = jnp.concatenate([column, column], axis=0).astype(BF16)
    own = dir_ref[:, 0, :]
    z_dir[0] = jnp.concatenate([own[:, :128], own[:, 128:256]], axis=0).astype(BF16)
    late[0, 0, 0, 0] = jnp.concatenate([own[:, 256:384], own[:, 384:]], axis=0).astype(BF16)

    def gather_z(buf, sem):
        for k in (4, 3, 5, 2, 6, 1, 7):
            remote(buf.at[0], buf.at[8 - k], sem, along(0, 0, k)).start()

    def gather_a2(buf, sem):
        for k in (2, 1, 3):
            remote(buf.at[0, 0, 0], buf.at[0, 0, 4 - k], sem, along(0, k, 0)).start()

    def spread(buf, k, lo, count, sem):
        part = pl.ds(lo, count)
        remote(buf.at[0, 0, part], buf.at[0, 4 - k, part], sem, along(k, 0, 0)).start()

    def to_sibling(buf, off, sem):
        remote(buf.at[0, off], buf.at[1, off], sem, sibling).start()

    def unpack(zbuf, buf):
        raw = zbuf[...].astype(F32)
        tiles = zbuf.shape[2] // 256 * 4 or 2
        width = tiles * 64
        halves = (raw[:, :8, :width].reshape(BLOCK, width), raw[:, 8:, :width].reshape(BLOCK, width))
        for k in range(tiles):
            lane = k * 128 % width
            piece = halves[k // (tiles // 2)][:, lane : lane + 128]
            buf[0, 0, 0, k * BLOCK : (k + 1) * BLOCK, :] = piece.astype(BF16)
        if zbuf.shape[2] > 256:
            bias = raw[:, :8, 256:].reshape(BLOCK, 128)
            row_at = lax.broadcasted_iota(jnp.int32, (BLOCK, 128), 0)
            lane_at = lax.broadcasted_iota(jnp.int32, (BLOCK, 128), 1) % BLOCK
            total = jnp.sum(jnp.where(row_at == lane_at, bias, 0.0), axis=0, keepdims=True)
            buf[0, 0, 0, CROWS:, :] = jnp.broadcast_to(total, (16, 128)).astype(BF16)

    def chunk_tile(buf, h, s, tiles=4):
        return jnp.concatenate(
            [buf[h, s, :, k * BLOCK : (k + 1) * BLOCK, :].reshape(TILE, 128) for k in range(tiles)], axis=1
        )

    def late_tile(h, s):
        raw = late[h, :, s].astype(F32)
        sides = [
            jnp.concatenate([raw[kz, k2, lo : lo + 8] for k2 in range(4) for kz in range(8)], axis=0)
            for lo in (0, 8)
        ]
        return jnp.concatenate(sides, axis=1).astype(BF16)

    def bias_tile(h, s):
        rows = w_high[h, s, :, CROWS:, :].astype(F32)
        lane = lax.broadcasted_iota(jnp.int32, (16, 128), 1)
        lines = [jnp.where(lane < BLOCK, rows[2 * k], rows[2 * k + 1])[:1] for k in range(2)]
        return jnp.concatenate(lines, axis=1)

    def two_tiles(row, j):
        return jnp.where(
            low_rows((8, 128)),
            jnp.broadcast_to(row[:, 2 * j * 128 : (2 * j + 1) * 128], (8, 128)),
            jnp.broadcast_to(row[:, (2 * j + 1) * 128 : (2 * j + 2) * 128], (8, 128)),
        )

    def conv_rows(first):
        @pl.loop(0, 4)
        def _(j):
            for r in (first, first + 1):
                acc = [None] * SIDE
                for kh in range(KER):
                    source = r + kh - KER // 2
                    if source < 0 or source >= SIDE:
                        continue
                    line = [taps[j, kh * KER + kw] for kw in range(KER)]
                    for col in range(SIDE):
                        value = pixels[j, source * SIDE + col]
                        for kw in range(KER):
                            to = col - kw + KER // 2
                            if 0 <= to < SIDE:
                                term = value * line[kw]
                                acc[to] = term if acc[to] is None else acc[to] + term
                shift = scales[0, j]
                for col in range(SIDE):
                    mixed[j, (r - first) * SIDE + col] = acc[col] + shift

    def norm_rows(first):
        parts = [mixed[j] for j in range(4)]
        total = jnp.sum(folded(parts[0] + parts[1] + parts[2] + parts[3]), axis=2, keepdims=True)
        average = total * (1.0 / CH)
        parts = [part - average for part in parts]
        squares = [part * part for part in parts]
        total = jnp.sum(folded(squares[0] + squares[1] + squares[2] + squares[3]), axis=2, keepdims=True)
        rstd = lax.rsqrt(total * (1.0 / CH) + 1e-06)
        lo = first * SIDE * IMGS
        for j in range(4):
            values = unzip(parts[j] * rstd * scales[1, j] + scales[2, j])
            for k in range(2):
                lane = (2 * j + k) * 128
                normed[lo : lo + PAIR * IMGS, lane : lane + 128] = (
                    values[k].reshape(PAIR * IMGS, 128).astype(BF16)
                )

    chunks = ((z_low, w_low, 0), (z_high, w_high, 20), (z_dir, w_dir, 40))
    LOW, HIGH, DIR = chunks

    def conv(first):
        conv_rows(first)
        norm_rows(first)

    def after_z(chunk):
        zbuf, buf, sem = chunk
        arrived(sem, zbuf.at[pl.ds(1, 7)])
        unpack(zbuf, buf)
        gather_a2(buf, sem + 1)
        if chunk is not DIR:
            spread(buf, 1, 0, 1, sem + 2)
            spread(buf, 3, 0, 1, sem + 3)

    def after_a2(chunk):
        _, buf, sem = chunk
        arrived(sem + 1, buf.at[0, 0, pl.ds(1, 3)])
        if chunk is DIR:
            for k in (1, 3, 2):
                spread(buf, k, 0, 4, sem + 1 + k)
        else:
            spread(buf, 1, 1, 3, sem + 4)
            spread(buf, 3, 1, 3, sem + 5)
        to_sibling(buf, 0, sem + 6)

    def after_a3(chunk):
        _, buf, sem = chunk
        arrived(sem + 2, buf.at[0, 3, pl.ds(0, 1)])
        arrived(sem + 4, buf.at[0, 3, pl.ds(1, 3)])
        remote(buf.at[0, 3, pl.ds(0, 2)], buf.at[0, 2, pl.ds(0, 2)], sem + 10, along(1, 0, 0)).start()
        arrived(sem + 3, buf.at[0, 1, pl.ds(0, 1)])
        arrived(sem + 5, buf.at[0, 1, pl.ds(1, 3)])
        remote(buf.at[0, 1, pl.ds(2, 2)], buf.at[0, 2, pl.ds(2, 2)], sem + 11, along(3, 0, 0)).start()
        to_sibling(buf, 3, sem + 9)
        to_sibling(buf, 1, sem + 7)

    def after_forward(chunk):
        _, buf, sem = chunk
        arrived(sem + 10, buf.at[0, 2, pl.ds(0, 2)])
        arrived(sem + 11, buf.at[0, 2, pl.ds(2, 2)])
        to_sibling(buf, 2, sem + 8)

    def from_sibling(chunk, off):
        _, buf, sem = chunk
        arrived(sem + 6 + off, buf.at[1, off])

    def project(p, h, s):
        weights = jnp.concatenate([chunk_tile(w_low, h, s), chunk_tile(w_high, h, s)], axis=1)
        pre = lax.dot_general(
            normed[...], weights, (((1,), (1,)), ((), ())), preferred_element_type=F32
        )
        hidden[:, p * TILE : (p + 1) * TILE] = gelu(pre + bias_tile(h, s)).astype(BF16)

    places = [(0, 0), (1, 0), (0, 3), (1, 3), (0, 1), (1, 1), (0, 2), (1, 2)]

    pl.semaphore_wait(barrier, 30)
    L = 60
    for k in range(1, 4):
        remote(late.at[0, 0, 0, 0], late.at[0, 0, 0, 4 - k], L, along(0, k, 0)).start()
    for zbuf, _, sem in chunks:
        gather_z(zbuf, sem)

    loads[1].wait()

    @pl.loop(0, KER)
    def _(kh):
        for kw in range(KER):
            line = kernel[kh, kw : kw + 1, :]
            for j in range(4):
                taps[j, kh * KER + kw] = two_tiles(line, j)

    for j in range(4):
        scales[0, j] = two_tiles(dw_bias_ref[...], j)
        scales[1, j] = two_tiles(gain_ref[...], j)
        scales[2, j] = two_tiles(ln_bias_ref[...], j)

    loads[0].wait()

    @pl.loop(0, SIDE)
    def _(r):
        cells = pl.ds(r * SIDE, SIDE)
        for j in range(2):
            block = images[cells, 16 * j : 16 * j + 16, :].astype(F32)
            pixels[2 * j, cells] = block[:, :8]
            pixels[2 * j + 1, cells] = block[:, 8:]

    conv(0)
    conv(2)
    arrived(L, late.at[0, 0, 0, pl.ds(1, 3)])
    for k in range(1, 4):
        remote(late.at[0, 0, 0], late.at[0, 0, 4 - k], L + 1, along(k, 0, 0)).start()
    conv(4)
    after_z(LOW)
    after_z(HIGH)
    arrived(L + 1, late.at[0, 0, pl.ds(1, 3)])
    for k in (4, 3, 5, 2, 6, 1, 7):
        remote(late.at[0, 0], late.at[0, 8 - k], L + 2, along(0, 0, k)).start()
    conv(6)
    after_z(DIR)
    conv(8)
    after_a2(LOW)
    conv(10)
    after_a2(HIGH)
    conv(12)
    after_a2(DIR)

    loads[2].wait()
    for k in range(2):
        root = roots[:, 8 * k : 8 * k + 8, :]
        first, second = unzip(0.25 + root * root)
        curvature[2 * k] = first
        curvature[2 * k + 1] = second

    project(0, 0, 0)
    after_a3(LOW)
    from_sibling(LOW, 0)
    from_sibling(HIGH, 0)
    project(1, 1, 0)
    after_a3(HIGH)
    project(2, 0, 3)
    project(4, 0, 1)
    arrived(L + 2, late.at[0, pl.ds(1, 7)])
    remote(late.at[0], late.at[1], L + 3, sibling).start()
    for k in (1, 3, 2):
        arrived(40 + 1 + k, w_dir.at[0, 4 - k])
        to_sibling(w_dir, 4 - k, 40 + 6 + 4 - k)
    after_forward(LOW)
    for off in (3, 1):
        from_sibling(LOW, off)
        from_sibling(HIGH, off)
    project(3, 1, 3)
    project(5, 1, 1)

    def direction_tile(h, s):
        return jnp.concatenate([chunk_tile(w_dir, h, s, 2), late_tile(h, s)], axis=1)

    def partial(lo, hi):
        directions = jnp.concatenate([direction_tile(h, s) for h, s in places[lo:hi]], axis=0)
        return jnp.dot(hidden[:, lo * TILE : hi * TILE], directions, preferred_element_type=F32)

    after_forward(HIGH)
    for off in range(4):
        from_sibling(DIR, off)
    arrived(L + 3, late.at[1])
    cell_out[...] = partial(0, 6)
    project(6, 0, 2)
    from_sibling(LOW, 2)
    from_sibling(HIGH, 2)
    project(7, 1, 2)
    cell_out[...] += partial(6, 8)

    scale = gamma_ref[...] * gamma_ref[...]
    for k in range(4):
        lanes = slice(k * 128, (k + 1) * 128)
        values = cell_out[:, lanes].reshape(CELLS // 2, 8, 128)
        mean = folded(jnp.sum(values, axis=0)) * (1.0 / CELLS)
        inner = curvature[k] * (values - mean)
        again = folded(jnp.sum(inner, axis=0)) * (1.0 / CELLS)
        final = (inner - again) * scale[:, lanes]
        cell_weight[:, lanes] = final.reshape(ROWS, 128).astype(BF16)

    def product(h, s):
        p = places.index((h, s))
        return lax.dot_general(
            hidden[:, p * TILE : (p + 1) * TILE],
            cell_weight[...],
            (((0,), (0,)), ((), ())),
            preferred_element_type=F32,
        )

    R = 64
    for off in (2, 1, 3, 0):
        pair_send[off] = product(1, off).astype(BF16)
        remote(pair_send.at[off], pair_recv.at[off], R + off, sibling).start()
    onward, home = pl.ds(1, 3), pl.ds(0, 1)
    for off in (2, 1, 3):
        part = product(0, off)
        arrived(R + off, pair_recv.at[off])
        part = part + pair_recv[off].astype(F32)
        slab_send[off - 1] = part.reshape(4, BLOCK, OUTC).astype(BF16)
        place = slab_recv.at[off - 1, onward]
        remote(slab_send.at[off - 1, onward], place, R + 3 + off, along(off, 0, 0)).start()
    for off in (2, 1, 3):
        place = slab_recv.at[off - 1, home]
        remote(slab_send.at[off - 1, home], place, R + 6 + off, along(off, 0, 0)).start()
    part = product(0, 0)
    arrived(R, pair_recv.at[0])
    kept[...] = (part + pair_recv[0].astype(F32)).reshape(4, BLOCK, OUTC)
    for off in (1, 3, 2):
        arrived(R + 3 + off, slab_recv.at[off - 1, onward])
    for k in (2, 1, 3):
        block = kept[k]
        for off in (1, 2, 3):
            block = block + slab_recv[off - 1, k].astype(F32)
        block_send[k - 1] = block.astype(BF16)
        remote(block_send.at[k - 1], block_recv.at[k - 1], R + 9 + k, along(0, k, 0)).start()
    block = kept[0]
    for off in (1, 3, 2):
        arrived(R + 6 + off, slab_recv.at[off - 1, home])
        block = block + slab_recv[off - 1, 0].astype(F32)
    for off in (1, 3, 2):
        arrived(R + 9 + off, block_recv.at[off - 1])
        block = block + block_recv[off - 1].astype(F32)
    rows = block.reshape(8, UNITS, OUTC)
    for k in (4, 3, 5, 2, 6, 1, 7):
        row_send[k - 1] = jnp.concatenate([rows[k, :, :256], rows[k, :, 256:]], axis=0).astype(BF16)
        remote(row_send.at[k - 1], row_recv.at[k - 1], R + 13, along(0, 0, k)).start()
    arrived(R + 13, row_recv)
    others = jnp.sum(row_recv[...].astype(F32), axis=0)
    summed = rows[0] + jnp.concatenate([others[:8], others[8:]], axis=1)

    N = R + 14
    estimate = dir_ref[:, 0, :]
    fresh = estimate + (1.0 - damping) * estimate - summed * (1.0 / (scale_coef * ALL_CELLS))
    fresh_part = jnp.sum(fresh * fresh, axis=(0, 1), keepdims=True)
    direction_part = jnp.sum(estimate * estimate, axis=(0, 1), keepdims=True)
    row = lax.broadcasted_iota(jnp.int32, (8, 128), 0)
    sums[...] = jnp.where(row < 4, fresh_part, direction_part)
    for k in FAR_FIRST:
        remote(sums, sums_recv.at[k - 1], N, group_of(k)).start()
    arrived(N, sums_recv)
    wide_sums[...] = sums[...] + jnp.sum(sums_recv[...], axis=0)
    for k in PLANE_FAR_FIRST:
        remote(wide_sums, wide_recv.at[k - 1], N + 1, plane_of(k)).start()
    arrived(N + 1, wide_recv)
    sq = wide_sums[...] + jnp.sum(wide_recv[...], axis=0)
    fresh_sq = sq[0:1, 0:1]
    direction_sq = sq[4:5, 0:1]
    factor = jnp.minimum(1.0, clip_ratio * jnp.sqrt(direction_sq / (fresh_sq + 1e-06)))
    out_ref[...] = fresh * factor

    for zbuf, buf, base in chunks:
        left(base, zbuf.at[pl.ds(1, 7)])
        left(base + 1, buf.at[0, 0, pl.ds(1, 3)])
        for off in range(4):
            left(base + 6 + off, buf.at[0, off])
    for _, buf, base in (LOW, HIGH):
        for k in range(2):
            left(base + 2 + k, buf.at[0, 0, pl.ds(0, 1)])
            left(base + 4 + k, buf.at[0, 0, pl.ds(1, 3)])
            left(base + 10 + k, buf.at[0, 0, pl.ds(0, 2)])
    for k in (1, 3, 2):
        left(40 + 1 + k, w_dir.at[0, 0])
    left(L, late.at[0, 0, 0, pl.ds(1, 3)])
    left(L + 1, late.at[0, 0, pl.ds(1, 3)])
    left(L + 2, late.at[0, pl.ds(1, 7)])
    left(L + 3, late.at[0])
    for off in range(4):
        left(R + off, pair_send.at[off])
    for off in range(1, 4):
        left(R + 3 + off, slab_send.at[off - 1, onward])
        left(R + 6 + off, slab_send.at[off - 1, home])
        left(R + 9 + off, block_send.at[off - 1])
    left(R + 13, row_recv)
    left(N, sums_recv)
    left(N + 1, wide_recv)


def step(*operands):
    vmem = pl.BlockSpec(memory_space=pltpu.VMEM)
    hbm = pl.BlockSpec(memory_space=pl.ANY)
    return pl.pallas_call(
        body,
        out_shape=jax.ShapeDtypeStruct((UNITS, OUTC), F32),
        in_specs=[hbm, hbm, vmem, vmem, vmem, vmem, vmem, vmem, hbm, vmem],
        out_specs=vmem,
        scratch_shapes=[
            pltpu.VMEM((CELLS, 32, 128), BF16),
            pltpu.VMEM((KER, KER, CH), F32),
            pltpu.VMEM((CELLS, 16, 128), F32),
            pltpu.VMEM((4, CELLS, 8, 128), F32),
            pltpu.VMEM((4, KER * KER, 8, 128), F32),
            pltpu.VMEM((3, 4, 8, 128), F32),
            pltpu.VMEM((4, PAIR, 8, 128), F32),
            pltpu.VMEM((ROWS, CH), BF16),
            pltpu.VMEM((4, CELLS // 2, 8, 128), F32),
            pltpu.VMEM((8, 16, 256), BF16),
            pltpu.VMEM((8, 16, 384), BF16),
            pltpu.VMEM((8, 16, 128), BF16),
            pltpu.VMEM((2, 4, 4, CROWS, 128), BF16),
            pltpu.VMEM((2, 4, 4, CROWS + 16, 128), BF16),
            pltpu.VMEM((2, 4, 4, CROWS // 2, 128), BF16),
            pltpu.VMEM((2, 8, 4, 4, 16, 128), BF16),
            pltpu.VMEM((ROWS, HID), BF16),
            pltpu.VMEM((ROWS, OUTC), F32),
            pltpu.VMEM((ROWS, OUTC), BF16),
            pltpu.VMEM((4, TILE, OUTC), BF16),
            pltpu.VMEM((4, TILE, OUTC), BF16),
            pltpu.VMEM((3, 4, BLOCK, OUTC), BF16),
            pltpu.VMEM((3, 4, BLOCK, OUTC), BF16),
            pltpu.VMEM((4, BLOCK, OUTC), F32),
            pltpu.VMEM((3, BLOCK, OUTC), BF16),
            pltpu.VMEM((3, BLOCK, OUTC), BF16),
            pltpu.VMEM((7, 16, 256), BF16),
            pltpu.VMEM((7, 16, 256), BF16),
            pltpu.VMEM((8, 128), F32),
            pltpu.VMEM((15, 8, 128), F32),
            pltpu.VMEM((8, 128), F32),
            pltpu.VMEM((15, 8, 128), F32),
            pltpu.SemaphoreType.DMA((96,)),
            pltpu.SemaphoreType.DMA((96,)),
            pltpu.SemaphoreType.DMA((3,)),
        ],
        compiler_params=pltpu.CompilerParams(
            collective_id=0, has_side_effects=True, vmem_limit_bytes=56 * 1024 * 1024
        ),
    )(*operands)


def cell_major(array):
    tiles = array.shape[3] // 128
    cells = array.transpose(1, 2, 0, 3).reshape(CELLS, IMGS, tiles, 128)
    return cells.transpose(0, 2, 1, 3).reshape(CELLS, tiles * IMGS, 128)


def per_device(
    images, dw_weight, dw_bias, ln_gain, ln_bias, w_in, b_in, gamma, curv_root, directions
):
    out = step(
        cell_major(images),
        dw_weight,
        dw_bias.reshape(1, CH),
        ln_gain.reshape(1, CH),
        ln_bias.reshape(1, CH),
        w_in.T.reshape(UNITS, 4, 256).transpose(1, 0, 2).reshape(32, 256),
        b_in.reshape(1, UNITS),
        gamma.reshape(1, OUTC),
        cell_major(curv_root),
        directions,
    )
    return out.reshape(UNITS, 1, OUTC)


def solution(mesh):
    placed = (
        P(("wide", "narrow"), None, None, None),
        P(),
        P(),
        P(),
        P(),
        P(None, ("wide", "narrow")),
        P(("wide", "narrow")),
        P(),
        P(("wide", "narrow"), None, None, None),
        P(("wide", "narrow"), None, None),
    )
    return jax.shard_map(
        per_device,
        mesh=mesh,
        in_specs=placed,
        out_specs=P(("wide", "narrow"), None, None),
        check_vma=False,
    )
```

```python
import jax
import jax.numpy as jnp
from jax import lax
from jax.experimental import pallas as pl
from jax.experimental.pallas import tpu as pltpu
from jax.sharding import PartitionSpec as P

damping = 0.05
scale_coef = 0.4
clip_ratio = 1.2

MESH = pl.DeviceIdType.MESH
F32 = jnp.float32
BF16 = jnp.bfloat16

CH = 1024
HID = 2048
OUTC = 512
SIDE = 14
KER = 7
IMGS = 4
CELLS = SIDE * SIDE
ROWS = IMGS * CELLS
ALL_CELLS = 1024 * CELLS
UNITS = 8
BLOCK = 64
CROWS = 4 * BLOCK
TILE = 256
FAR_FIRST = (8, 7, 9, 6, 10, 5, 11, 4, 12, 3, 13, 2, 14, 1, 15)
PLANE_FAR_FIRST = (10, 9, 11, 6, 14, 5, 7, 13, 15, 2, 8, 1, 3, 4, 12)
PAIR = 2 * SIDE


def gelu(pre):
    return 0.5 * pre * (1.0 + lax.erf(pre * 0.7071067811865476))


def low_rows(shape):
    return lax.broadcasted_iota(jnp.int32, shape, len(shape) - 2) < 4


def folded(values):
    return values + pltpu.roll(values, 4, values.ndim - 2)


def unzip(values):
    count = values.shape[0] // 2
    pairs = values.reshape(count, 2, 8, 128)
    even, odd = pairs[:, 0], pairs[:, 1]
    low = low_rows((count, 8, 128))
    return (
        jnp.where(low, even, pltpu.roll(odd, 4, 1)),
        jnp.where(low, pltpu.roll(even, 4, 1), odd),
    )


def body(
    images_hbm,
    kernel_hbm,
    dw_bias_ref,
    gain_ref,
    ln_bias_ref,
    w_ref,
    b_ref,
    gamma_ref,
    curv_hbm,
    dir_ref,
    out_ref,
    images,
    kernel,
    roots,
    pixels,
    taps,
    scales,
    mixed,
    normed,
    curvature,
    z_low,
    z_high,
    z_dir,
    w_low,
    w_high,
    w_dir,
    late,
    hidden,
    cell_out,
    cell_weight,
    pair_send,
    pair_recv,
    slab_send,
    slab_recv,
    kept,
    block_send,
    block_recv,
    row_send,
    row_recv,
    sums,
    sums_recv,
    wide_sums,
    wide_recv,
    send,
    recv,
    load,
):
    loads = [
        pltpu.make_async_copy(images_hbm, images, load.at[0]),
        pltpu.make_async_copy(kernel_hbm, kernel, load.at[1]),
        pltpu.make_async_copy(curv_hbm, roots, load.at[2]),
    ]
    for copy in loads:
        copy.start()

    wide = lax.axis_index("wide")
    narrow = lax.axis_index("narrow")
    x = wide // 16
    z = (wide // 2) % 8
    y = (wide % 2) * 2 + narrow // 2
    c = narrow % 2
    a3 = x + c * (y - x)
    a2 = y + c * (x - y)

    def at(x_, y_, z_, c_):
        return ((x_ * 8 + z_) * 2 + y_ // 2, (y_ % 2) * 2 + c_)

    def along(k3, k2, kz):
        a3_ = (a3 + k3) % 4
        a2_ = (a2 + k2) % 4
        return at(a3_ + c * (a2_ - a3_), a2_ + c * (a3_ - a2_), (z + kz) % 8, c)

    sibling = at(x, y, z, 1 - c)

    def group_of(k):
        spot = (z * 2 + c + k) % 16
        return at(x, y, spot // 2, spot % 2)

    def plane_of(k):
        spot = (x * 4 + y + k) % 16
        return at(spot // 4, spot % 4, z, c)

    def remote(src, dst, sem, device):
        return pltpu.make_async_remote_copy(
            src_ref=src,
            dst_ref=dst,
            send_sem=send.at[sem],
            recv_sem=recv.at[sem],
            device_id=device,
            device_id_type=MESH,
        )

    def arrived(sem, ref):
        pltpu.make_async_copy(ref, ref, recv.at[sem]).wait()

    def left(sem, ref):
        pltpu.make_async_copy(ref, ref, send.at[sem]).wait()

    barrier = pltpu.get_barrier_semaphore()
    for k in FAR_FIRST:
        pl.semaphore_signal(barrier, inc=1, device_id=group_of(k), device_id_type=MESH)
        pl.semaphore_signal(barrier, inc=1, device_id=plane_of(k), device_id_type=MESH)

    z_low[0] = w_ref[0:16, :]
    z_high[0, :, 0:256] = w_ref[16:32, :]
    row8 = lax.broadcasted_iota(jnp.int32, (8, 8), 0)
    lane8 = lax.broadcasted_iota(jnp.int32, (8, 8), 1)
    line = jnp.broadcast_to(b_ref[...].astype(F32), (8, 8))
    column = jnp.sum(jnp.where(row8 == lane8, line, 0.0), axis=1, keepdims=True)
    column = jnp.broadcast_to(column, (8, 128))
    z_high[0, :, 256:384] = jnp.concatenate([column, column], axis=0).astype(BF16)
    own = dir_ref[:, 0, :]
    z_dir[0] = jnp.concatenate([own[:, :128], own[:, 128:256]], axis=0).astype(BF16)
    late[0, 0, 0, 0] = jnp.concatenate([own[:, 256:384], own[:, 384:]], axis=0).astype(BF16)

    def gather_z(buf, sem):
        for k in (4, 3, 5, 2, 6, 1, 7):
            remote(buf.at[0], buf.at[8 - k], sem, along(0, 0, k)).start()

    def gather_a2(buf, sem):
        for k in (2, 1, 3):
            remote(buf.at[0, 0, 0], buf.at[0, 0, 4 - k], sem, along(0, k, 0)).start()

    def spread(buf, k, lo, count, sem):
        part = pl.ds(lo, count)
        remote(buf.at[0, 0, part], buf.at[0, 4 - k, part], sem, along(k, 0, 0)).start()

    def to_sibling(buf, off, sem):
        remote(buf.at[0, off], buf.at[1, off], sem, sibling).start()

    def unpack(zbuf, buf):
        raw = zbuf[...].astype(F32)
        tiles = zbuf.shape[2] // 256 * 4 or 2
        width = tiles * 64
        halves = (raw[:, :8, :width].reshape(BLOCK, width), raw[:, 8:, :width].reshape(BLOCK, width))
        for k in range(tiles):
            lane = k * 128 % width
            piece = halves[k // (tiles // 2)][:, lane : lane + 128]
            buf[0, 0, 0, k * BLOCK : (k + 1) * BLOCK, :] = piece.astype(BF16)
        if zbuf.shape[2] > 256:
            bias = raw[:, :8, 256:].reshape(BLOCK, 128)
            row_at = lax.broadcasted_iota(jnp.int32, (BLOCK, 128), 0)
            lane_at = lax.broadcasted_iota(jnp.int32, (BLOCK, 128), 1) % BLOCK
            total = jnp.sum(jnp.where(row_at == lane_at, bias, 0.0), axis=0, keepdims=True)
            buf[0, 0, 0, CROWS:, :] = jnp.broadcast_to(total, (16, 128)).astype(BF16)

    def chunk_tile(buf, h, s, tiles=4):
        return jnp.concatenate(
            [buf[h, s, :, k * BLOCK : (k + 1) * BLOCK, :].reshape(TILE, 128) for k in range(tiles)], axis=1
        )

    def late_tile(h, s):
        raw = late[h, :, s].astype(F32)
        sides = [
            jnp.concatenate([raw[kz, k2, lo : lo + 8] for k2 in range(4) for kz in range(8)], axis=0)
            for lo in (0, 8)
        ]
        return jnp.concatenate(sides, axis=1).astype(BF16)

    def bias_tile(h, s):
        rows = w_high[h, s, :, CROWS:, :].astype(F32)
        lane = lax.broadcasted_iota(jnp.int32, (16, 128), 1)
        lines = [jnp.where(lane < BLOCK, rows[2 * k], rows[2 * k + 1])[:1] for k in range(2)]
        return jnp.concatenate(lines, axis=1)

    def two_tiles(row, j):
        return jnp.where(
            low_rows((8, 128)),
            jnp.broadcast_to(row[:, 2 * j * 128 : (2 * j + 1) * 128], (8, 128)),
            jnp.broadcast_to(row[:, (2 * j + 1) * 128 : (2 * j + 2) * 128], (8, 128)),
        )

    def conv_rows(first):
        @pl.loop(0, 4)
        def _(j):
            for r in (first, first + 1):
                acc = [None] * SIDE
                for kh in range(KER):
                    source = r + kh - KER // 2
                    if source < 0 or source >= SIDE:
                        continue
                    line = [taps[j, kh * KER + kw] for kw in range(KER)]
                    for col in range(SIDE):
                        value = pixels[j, source * SIDE + col]
                        for kw in range(KER):
                            to = col - kw + KER // 2
                            if 0 <= to < SIDE:
                                term = value * line[kw]
                                acc[to] = term if acc[to] is None else acc[to] + term
                shift = scales[0, j]
                for col in range(SIDE):
                    mixed[j, (r - first) * SIDE + col] = acc[col] + shift

    def norm_rows(first):
        parts = [mixed[j] for j in range(4)]
        total = jnp.sum(folded(parts[0] + parts[1] + parts[2] + parts[3]), axis=2, keepdims=True)
        average = total * (1.0 / CH)
        parts = [part - average for part in parts]
        squares = [part * part for part in parts]
        total = jnp.sum(folded(squares[0] + squares[1] + squares[2] + squares[3]), axis=2, keepdims=True)
        rstd = lax.rsqrt(total * (1.0 / CH) + 1e-06)
        lo = first * SIDE * IMGS
        for j in range(4):
            values = unzip(parts[j] * rstd * scales[1, j] + scales[2, j])
            for k in range(2):
                lane = (2 * j + k) * 128
                normed[lo : lo + PAIR * IMGS, lane : lane + 128] = (
                    values[k].reshape(PAIR * IMGS, 128).astype(BF16)
                )

    chunks = ((z_low, w_low, 0), (z_high, w_high, 20), (z_dir, w_dir, 40))
    LOW, HIGH, DIR = chunks

    def conv(first):
        conv_rows(first)
        norm_rows(first)

    def after_z(chunk):
        zbuf, buf, sem = chunk
        arrived(sem, zbuf.at[pl.ds(1, 7)])
        unpack(zbuf, buf)
        gather_a2(buf, sem + 1)
        if chunk is not DIR:
            spread(buf, 1, 0, 1, sem + 2)
            spread(buf, 3, 0, 1, sem + 3)

    def after_a2(chunk):
        _, buf, sem = chunk
        arrived(sem + 1, buf.at[0, 0, pl.ds(1, 3)])
        if chunk is DIR:
            for k in (1, 3, 2):
                spread(buf, k, 0, 4, sem + 1 + k)
        else:
            spread(buf, 1, 1, 3, sem + 4)
            spread(buf, 3, 1, 3, sem + 5)
        to_sibling(buf, 0, sem + 6)

    def after_a3(chunk):
        _, buf, sem = chunk
        arrived(sem + 2, buf.at[0, 3, pl.ds(0, 1)])
        arrived(sem + 4, buf.at[0, 3, pl.ds(1, 3)])
        remote(buf.at[0, 3, pl.ds(0, 2)], buf.at[0, 2, pl.ds(0, 2)], sem + 10, along(1, 0, 0)).start()
        arrived(sem + 3, buf.at[0, 1, pl.ds(0, 1)])
        arrived(sem + 5, buf.at[0, 1, pl.ds(1, 3)])
        remote(buf.at[0, 1, pl.ds(2, 2)], buf.at[0, 2, pl.ds(2, 2)], sem + 11, along(3, 0, 0)).start()
        to_sibling(buf, 3, sem + 9)
        to_sibling(buf, 1, sem + 7)

    def after_forward(chunk):
        _, buf, sem = chunk
        arrived(sem + 10, buf.at[0, 2, pl.ds(0, 2)])
        arrived(sem + 11, buf.at[0, 2, pl.ds(2, 2)])
        to_sibling(buf, 2, sem + 8)

    def from_sibling(chunk, off):
        _, buf, sem = chunk
        arrived(sem + 6 + off, buf.at[1, off])

    def project(p, h, s):
        weights = jnp.concatenate([chunk_tile(w_low, h, s), chunk_tile(w_high, h, s)], axis=1)
        pre = lax.dot_general(
            normed[...], weights, (((1,), (1,)), ((), ())), preferred_element_type=F32
        )
        hidden[:, p * TILE : (p + 1) * TILE] = gelu(pre + bias_tile(h, s)).astype(BF16)

    places = [(0, 0), (1, 0), (0, 3), (1, 3), (0, 1), (1, 1), (0, 2), (1, 2)]

    pl.semaphore_wait(barrier, 30)
    L = 60
    for k in range(1, 4):
        remote(late.at[0, 0, 0, 0], late.at[0, 0, 0, 4 - k], L, along(0, k, 0)).start()
    for zbuf, _, sem in chunks:
        gather_z(zbuf, sem)

    loads[1].wait()

    @pl.loop(0, KER)
    def _(kh):
        for kw in range(KER):
            line = kernel[kh, kw : kw + 1, :]
            for j in range(4):
                taps[j, kh * KER + kw] = two_tiles(line, j)

    for j in range(4):
        scales[0, j] = two_tiles(dw_bias_ref[...], j)
        scales[1, j] = two_tiles(gain_ref[...], j)
        scales[2, j] = two_tiles(ln_bias_ref[...], j)

    loads[0].wait()

    @pl.loop(0, SIDE)
    def _(r):
        cells = pl.ds(r * SIDE, SIDE)
        for j in range(2):
            block = images[cells, 16 * j : 16 * j + 16, :].astype(F32)
            pixels[2 * j, cells] = block[:, :8]
            pixels[2 * j + 1, cells] = block[:, 8:]

    conv(0)
    conv(2)
    arrived(L, late.at[0, 0, 0, pl.ds(1, 3)])
    for k in range(1, 4):
        remote(late.at[0, 0, 0], late.at[0, 0, 4 - k], L + 1, along(k, 0, 0)).start()
    conv(4)
    after_z(LOW)
    after_z(HIGH)
    arrived(L + 1, late.at[0, 0, pl.ds(1, 3)])
    for k in (4, 3, 5, 2, 6, 1, 7):
        remote(late.at[0, 0], late.at[0, 8 - k], L + 2, along(0, 0, k)).start()
    conv(6)
    after_z(DIR)
    conv(8)
    after_a2(LOW)
    conv(10)
    after_a2(HIGH)
    conv(12)
    after_a2(DIR)

    loads[2].wait()
    for k in range(2):
        root = roots[:, 8 * k : 8 * k + 8, :]
        first, second = unzip(0.25 + root * root)
        curvature[2 * k] = first
        curvature[2 * k + 1] = second

    project(0, 0, 0)
    after_a3(LOW)
    from_sibling(LOW, 0)
    from_sibling(HIGH, 0)
    project(1, 1, 0)
    after_a3(HIGH)
    project(2, 0, 3)
    project(4, 0, 1)
    arrived(L + 2, late.at[0, pl.ds(1, 7)])
    remote(late.at[0], late.at[1], L + 3, sibling).start()
    for k in (1, 3, 2):
        arrived(40 + 1 + k, w_dir.at[0, 4 - k])
        to_sibling(w_dir, 4 - k, 40 + 6 + 4 - k)
    after_forward(LOW)
    for off in (3, 1):
        from_sibling(LOW, off)
        from_sibling(HIGH, off)
    project(3, 1, 3)
    project(5, 1, 1)

    def direction_tile(h, s):
        return jnp.concatenate([chunk_tile(w_dir, h, s, 2), late_tile(h, s)], axis=1)

    def partial(lo, hi):
        directions = jnp.concatenate([direction_tile(h, s) for h, s in places[lo:hi]], axis=0)
        return jnp.dot(hidden[:, lo * TILE : hi * TILE], directions, preferred_element_type=F32)

    after_forward(HIGH)
    for off in range(4):
        from_sibling(DIR, off)
    arrived(L + 3, late.at[1])
    project(6, 0, 2)
    cell_out[...] = partial(0, 7)
    from_sibling(LOW, 2)
    from_sibling(HIGH, 2)
    project(7, 1, 2)
    cell_out[...] += partial(7, 8)

    scale = gamma_ref[...] * gamma_ref[...]
    for k in range(4):
        lanes = slice(k * 128, (k + 1) * 128)
        values = cell_out[:, lanes].reshape(CELLS // 2, 8, 128)
        mean = folded(jnp.sum(values, axis=0)) * (1.0 / CELLS)
        inner = curvature[k] * (values - mean)
        again = folded(jnp.sum(inner, axis=0)) * (1.0 / CELLS)
        final = (inner - again) * scale[:, lanes]
        cell_weight[:, lanes] = final.reshape(ROWS, 128).astype(BF16)

    def product(h, s):
        p = places.index((h, s))
        return lax.dot_general(
            hidden[:, p * TILE : (p + 1) * TILE],
            cell_weight[...],
            (((0,), (0,)), ((), ())),
            preferred_element_type=F32,
        )

    R = 64
    for off in (2, 1, 3, 0):
        pair_send[off] = product(1, off).astype(BF16)
        remote(pair_send.at[off], pair_recv.at[off], R + off, sibling).start()
    onward, home = pl.ds(1, 3), pl.ds(0, 1)
    for off in (2, 1, 3):
        part = product(0, off)
        arrived(R + off, pair_recv.at[off])
        part = part + pair_recv[off].astype(F32)
        slab_send[off - 1] = part.reshape(4, BLOCK, OUTC).astype(BF16)
        place = slab_recv.at[off - 1, onward]
        remote(slab_send.at[off - 1, onward], place, R + 3 + off, along(off, 0, 0)).start()
    for off in (2, 1, 3):
        place = slab_recv.at[off - 1, home]
        remote(slab_send.at[off - 1, home], place, R + 6 + off, along(off, 0, 0)).start()
    part = product(0, 0)
    arrived(R, pair_recv.at[0])
    kept[...] = (part + pair_recv[0].astype(F32)).reshape(4, BLOCK, OUTC)
    for off in (1, 3, 2):
        arrived(R + 3 + off, slab_recv.at[off - 1, onward])
    for k in (2, 1, 3):
        block = kept[k]
        for off in (1, 2, 3):
            block = block + slab_recv[off - 1, k].astype(F32)
        block_send[k - 1] = block.astype(BF16)
        remote(block_send.at[k - 1], block_recv.at[k - 1], R + 9 + k, along(0, k, 0)).start()
    block = kept[0]
    for off in (1, 3, 2):
        arrived(R + 6 + off, slab_recv.at[off - 1, home])
        block = block + slab_recv[off - 1, 0].astype(F32)
    for off in (1, 3, 2):
        arrived(R + 9 + off, block_recv.at[off - 1])
        block = block + block_recv[off - 1].astype(F32)
    rows = block.reshape(8, UNITS, OUTC)
    for k in (4, 3, 5, 2, 6, 1, 7):
        row_send[k - 1] = jnp.concatenate([rows[k, :, :256], rows[k, :, 256:]], axis=0).astype(BF16)
        remote(row_send.at[k - 1], row_recv.at[k - 1], R + 13, along(0, 0, k)).start()
    arrived(R + 13, row_recv)
    others = jnp.sum(row_recv[...].astype(F32), axis=0)
    summed = rows[0] + jnp.concatenate([others[:8], others[8:]], axis=1)

    N = R + 14
    estimate = dir_ref[:, 0, :]
    fresh = estimate + (1.0 - damping) * estimate - summed * (1.0 / (scale_coef * ALL_CELLS))
    fresh_part = jnp.sum(fresh * fresh, axis=(0, 1), keepdims=True)
    direction_part = jnp.sum(estimate * estimate, axis=(0, 1), keepdims=True)
    row = lax.broadcasted_iota(jnp.int32, (8, 128), 0)
    sums[...] = jnp.where(row < 4, fresh_part, direction_part)
    for k in FAR_FIRST:
        remote(sums, sums_recv.at[k - 1], N, group_of(k)).start()
    arrived(N, sums_recv)
    wide_sums[...] = sums[...] + jnp.sum(sums_recv[...], axis=0)
    for k in PLANE_FAR_FIRST:
        remote(wide_sums, wide_recv.at[k - 1], N + 1, plane_of(k)).start()
    arrived(N + 1, wide_recv)
    sq = wide_sums[...] + jnp.sum(wide_recv[...], axis=0)
    fresh_sq = sq[0:1, 0:1]
    direction_sq = sq[4:5, 0:1]
    factor = jnp.minimum(1.0, clip_ratio * jnp.sqrt(direction_sq / (fresh_sq + 1e-06)))
    out_ref[...] = fresh * factor

    for zbuf, buf, base in chunks:
        left(base, zbuf.at[pl.ds(1, 7)])
        left(base + 1, buf.at[0, 0, pl.ds(1, 3)])
        for off in range(4):
            left(base + 6 + off, buf.at[0, off])
    for _, buf, base in (LOW, HIGH):
        for k in range(2):
            left(base + 2 + k, buf.at[0, 0, pl.ds(0, 1)])
            left(base + 4 + k, buf.at[0, 0, pl.ds(1, 3)])
            left(base + 10 + k, buf.at[0, 0, pl.ds(0, 2)])
    for k in (1, 3, 2):
        left(40 + 1 + k, w_dir.at[0, 0])
    left(L, late.at[0, 0, 0, pl.ds(1, 3)])
    left(L + 1, late.at[0, 0, pl.ds(1, 3)])
    left(L + 2, late.at[0, pl.ds(1, 7)])
    left(L + 3, late.at[0])
    for off in range(4):
        left(R + off, pair_send.at[off])
    for off in range(1, 4):
        left(R + 3 + off, slab_send.at[off - 1, onward])
        left(R + 6 + off, slab_send.at[off - 1, home])
        left(R + 9 + off, block_send.at[off - 1])
    left(R + 13, row_recv)
    left(N, sums_recv)
    left(N + 1, wide_recv)


def step(*operands):
    vmem = pl.BlockSpec(memory_space=pltpu.VMEM)
    hbm = pl.BlockSpec(memory_space=pl.ANY)
    return pl.pallas_call(
        body,
        out_shape=jax.ShapeDtypeStruct((UNITS, OUTC), F32),
        in_specs=[hbm, hbm, vmem, vmem, vmem, vmem, vmem, vmem, hbm, vmem],
        out_specs=vmem,
        scratch_shapes=[
            pltpu.VMEM((CELLS, 32, 128), BF16),
            pltpu.VMEM((KER, KER, CH), F32),
            pltpu.VMEM((CELLS, 16, 128), F32),
            pltpu.VMEM((4, CELLS, 8, 128), F32),
            pltpu.VMEM((4, KER * KER, 8, 128), F32),
            pltpu.VMEM((3, 4, 8, 128), F32),
            pltpu.VMEM((4, PAIR, 8, 128), F32),
            pltpu.VMEM((ROWS, CH), BF16),
            pltpu.VMEM((4, CELLS // 2, 8, 128), F32),
            pltpu.VMEM((8, 16, 256), BF16),
            pltpu.VMEM((8, 16, 384), BF16),
            pltpu.VMEM((8, 16, 128), BF16),
            pltpu.VMEM((2, 4, 4, CROWS, 128), BF16),
            pltpu.VMEM((2, 4, 4, CROWS + 16, 128), BF16),
            pltpu.VMEM((2, 4, 4, CROWS // 2, 128), BF16),
            pltpu.VMEM((2, 8, 4, 4, 16, 128), BF16),
            pltpu.VMEM((ROWS, HID), BF16),
            pltpu.VMEM((ROWS, OUTC), F32),
            pltpu.VMEM((ROWS, OUTC), BF16),
            pltpu.VMEM((4, TILE, OUTC), BF16),
            pltpu.VMEM((4, TILE, OUTC), BF16),
            pltpu.VMEM((3, 4, BLOCK, OUTC), BF16),
            pltpu.VMEM((3, 4, BLOCK, OUTC), BF16),
            pltpu.VMEM((4, BLOCK, OUTC), F32),
            pltpu.VMEM((3, BLOCK, OUTC), BF16),
            pltpu.VMEM((3, BLOCK, OUTC), BF16),
            pltpu.VMEM((7, 16, 256), BF16),
            pltpu.VMEM((7, 16, 256), BF16),
            pltpu.VMEM((8, 128), F32),
            pltpu.VMEM((15, 8, 128), F32),
            pltpu.VMEM((8, 128), F32),
            pltpu.VMEM((15, 8, 128), F32),
            pltpu.SemaphoreType.DMA((96,)),
            pltpu.SemaphoreType.DMA((96,)),
            pltpu.SemaphoreType.DMA((3,)),
        ],
        compiler_params=pltpu.CompilerParams(
            collective_id=0, has_side_effects=True, vmem_limit_bytes=56 * 1024 * 1024
        ),
    )(*operands)


def cell_major(array):
    tiles = array.shape[3] // 128
    cells = array.transpose(1, 2, 0, 3).reshape(CELLS, IMGS, tiles, 128)
    return cells.transpose(0, 2, 1, 3).reshape(CELLS, tiles * IMGS, 128)


def per_device(
    images, dw_weight, dw_bias, ln_gain, ln_bias, w_in, b_in, gamma, curv_root, directions
):
    out = step(
        cell_major(images),
        dw_weight,
        dw_bias.reshape(1, CH),
        ln_gain.reshape(1, CH),
        ln_bias.reshape(1, CH),
        w_in.T.reshape(UNITS, 4, 256).transpose(1, 0, 2).reshape(32, 256),
        b_in.reshape(1, UNITS),
        gamma.reshape(1, OUTC),
        cell_major(curv_root),
        directions,
    )
    return out.reshape(UNITS, 1, OUTC)


def solution(mesh):
    placed = (
        P(("wide", "narrow"), None, None, None),
        P(),
        P(),
        P(),
        P(),
        P(None, ("wide", "narrow")),
        P(("wide", "narrow")),
        P(),
        P(("wide", "narrow"), None, None, None),
        P(("wide", "narrow"), None, None),
    )
    return jax.shard_map(
        per_device,
        mesh=mesh,
        in_specs=placed,
        out_specs=P(("wide", "narrow"), None, None),
        check_vma=False,
    )
```
